32 devices in a mesh: case: 2 (over x), tile: 16 (over z, y, core).
Axes of the slice: x: 2, y: 2, z: 4, core: 2. Of those that a mesh axis runs over, the one named last changes fastest.
Arguments:
- segment_maps: bfloat16 [128, 256, 256], P(('case', 'tile')), parts along dimension 0, may hold values from -1.5 to 1.5
- cotangent: bfloat16 [768, 64, 64], P(('case', 'tile')), parts along dimension 0, may hold values from -6 to 6
- wavelengths: float32 [16], replicated, may hold values from 0.8 to 1.6
- intersections: int32 [512, 2, 5], P(('case', 'tile')), parts along dimension 0, may hold values from 0 to 192, as said below
Outputs:
- grad_maps: float32 [128, 256, 256], P(('case', 'tile')), parts along dimension 0
The draws below stay inside these ranges and needn't reach their ends.
There are 2 independent parts, one for each index of `case`. The reference program is written for one: setup_inputs(seed, part) draws one part's arguments, and reference() takes and returns one part's arrays. A program takes and returns all parts, laid end to end along the dimension named above; an argument that names none is the same for every part. Nothing has to cross between parts.
Inputs may be any that keep to these rules, and one draw needn't show every extreme that they name: `intersections`: column 0 is 0 or 1; column 1 is below 4, column 2 below 24, columns 3 and 4 at most 192. In every draw one tile receives 2 live slots from every segment owner.
All inputs are finite; a program needn't handle non-finite values.
Results may differ from the reference program's by a relative error of at most 0.0046.
Values may be sent and summed in bfloat16 or wider, within the bound.
No kernel may reach another device: no remote copies, remote signals or barrier semaphores. Data moves between devices by JAX's collectives and lax.ppermute only.
A program may use at most 64 MiB of HBM per device.

```python
import math
import jax
import jax.numpy as jnp
from jax import lax

SEG_PX = 256
SUB = 64
FOC = 64
NW = 16
CAP = 2
SEG_DEV = 4
LENS_DEV = 24
PEERS = 16
SEGMENTS = 64
LENSES = 384
N_TILE = 16


def draw_intersections(key, part):
    key = jax.random.fold_in(key, 7)
    keys = jax.random.split(key, 6)
    shape = (PEERS * PEERS, CAP)
    busiest = jax.random.randint(keys[0], (), 0, PEERS)
    target = (jnp.arange(PEERS * PEERS, dtype=jnp.int32) % PEERS)[:, None]
    usable = (jax.random.randint(keys[1], shape, 0, 100) < 40) | (target == busiest)
    usable = usable.astype(jnp.int32)
    segment_ids = jax.random.randint(keys[2], shape, 0, SEG_DEV)
    lens_ids = jax.random.randint(keys[3], shape, 0, LENS_DEV)
    row_offs = jax.random.randint(keys[4], shape, 0, SEG_PX - SUB + 1)
    col_offs = jax.random.randint(keys[5], shape, 0, SEG_PX - SUB + 1)
    return jnp.stack([usable, segment_ids, lens_ids, row_offs, col_offs], axis=-1).astype(jnp.int32)


def level_of(key, dims, pieces, low, high):
    loudness = 1.0
    for axis_at, blocks in pieces:
        heights = jax.random.uniform(jax.random.fold_in(jax.random.fold_in(key, 6), axis_at), (blocks,), jnp.float32, low / len(pieces), high / len(pieces))
        loudness = loudness * jnp.repeat(jnp.exp(heights), dims[axis_at] // blocks).reshape((-1,) + (1,) * (len(dims) - 1 - axis_at))
    return loudness


def noise(own_key, shape, spread, limit, pieces=(), kind=jnp.bfloat16):
    values = jax.random.normal(own_key, shape, jnp.float32) * spread
    if len(pieces) > 0:
        values = level_of(own_key, shape, pieces, -0.22, 0.18) * values
    return jnp.clip(values, min=-limit, max=limit).astype(kind)


def setup_inputs(seed: int = 0, part: int = 0) -> dict:
    seeds = jax.random.split(jax.random.key(seed), 5)
    part_keys = jax.random.split(jax.random.fold_in(seeds[4], part), 5)
    segment_maps = noise(part_keys[0], (SEGMENTS, SEG_PX, SEG_PX), 0.25, 1.5, ((0, 16),))
    cotangent = noise(part_keys[1], (LENSES, FOC, FOC), 1.0, 6.0, ((0, 16),))
    wavelengths = jnp.clip(jnp.exp(jax.random.uniform(seeds[2], (NW,), jnp.float32, math.log(0.8), math.log(1.6))), 0.8, 1.6)
    intersections = draw_intersections(jax.random.fold_in(jax.random.fold_in(seeds[4], part), 71), part)
    return dict(segment_maps=segment_maps, cotangent=cotangent, wavelengths=wavelengths, intersections=intersections)


SAMPLING = 0.5
TWO_PI = 2.0 * math.pi

def hex_mask(extent):
    across = jnp.abs(2 * jnp.arange(extent, dtype=jnp.int32) - (extent - 1))
    down = across[:, None]
    sideways = across[None, :]
    inside = (8 * down <= 7 * (extent - 1)) & (7 * sideways + 4 * down <= 7 * (extent - 1))
    return inside.astype(jnp.bfloat16)

def lens_tables(wavelength, focal, pupil):
    focal_pos = jnp.arange(focal, dtype=jnp.int32) - focal // 2
    pupil_pos = jnp.arange(pupil, dtype=jnp.int32) - pupil // 2
    product = (focal_pos[:, None] * pupil_pos[None, :]).astype(jnp.float32)
    angles = product * (-TWO_PI * SAMPLING / pupil) / wavelength
    return (jnp.cos(angles).astype(jnp.bfloat16), jnp.sin(angles).astype(jnp.bfloat16))

def wave_grad(opd, amplitude, cotangent, wavelength, waves):
    real_tab, imag_tab = lens_tables(wavelength, FOC, SUB)
    real_f = real_tab.astype(jnp.float32)
    imag_f = imag_tab.astype(jnp.float32)
    phase = TWO_PI / wavelength * opd
    cosine = jnp.cos(phase)
    sine = jnp.sin(phase)
    field_re = (amplitude * cosine).astype(jnp.bfloat16).astype(jnp.float32)
    field_im = (amplitude * sine).astype(jnp.bfloat16).astype(jnp.float32)
    left_re = (jnp.einsum('ux,lxy->luy', real_f, field_re) - jnp.einsum('ux,lxy->luy', imag_f, field_im)).astype(jnp.bfloat16).astype(jnp.float32)
    left_im = (jnp.einsum('ux,lxy->luy', real_f, field_im) + jnp.einsum('ux,lxy->luy', imag_f, field_re)).astype(jnp.bfloat16).astype(jnp.float32)
    image_re = (jnp.einsum('luy,vy->luv', left_re, real_f) - jnp.einsum('luy,vy->luv', left_im, imag_f)) / SUB
    image_im = (jnp.einsum('luy,vy->luv', left_re, imag_f) + jnp.einsum('luy,vy->luv', left_im, real_f)) / SUB
    weight = cotangent.astype(jnp.float32) * (2.0 / waves)
    hold_re = (weight * image_re).astype(jnp.bfloat16).astype(jnp.float32)
    hold_im = (weight * image_im).astype(jnp.bfloat16).astype(jnp.float32)
    back_re = (jnp.einsum('ux,luv->lxv', real_f, hold_re) + jnp.einsum('ux,luv->lxv', imag_f, hold_im)).astype(jnp.bfloat16).astype(jnp.float32)
    back_im = (jnp.einsum('ux,luv->lxv', real_f, hold_im) - jnp.einsum('ux,luv->lxv', imag_f, hold_re)).astype(jnp.bfloat16).astype(jnp.float32)
    grad_re = (jnp.einsum('lxv,vy->lxy', back_re, real_f) + jnp.einsum('lxv,vy->lxy', back_im, imag_f)) / SUB
    grad_im = (jnp.einsum('lxv,vy->lxy', back_im, real_f) - jnp.einsum('lxv,vy->lxy', back_re, imag_f)) / SUB
    return TWO_PI / wavelength * amplitude * (cosine * grad_im - sine * grad_re)

def reference(segment_maps, cotangent, wavelengths, intersections):
    peers = N_TILE
    entries = intersections.reshape(-1, 5)
    count = entries.shape[0]
    slot_ids = jnp.arange(count, dtype=jnp.int32)
    source = slot_ids // (peers * CAP)
    target = slot_ids // CAP % peers
    usable = entries[:, 0]
    segment_ids = (source * SEG_DEV + entries[:, 1]).astype(jnp.int32)
    lens_ids = (target * LENS_DEV + entries[:, 2]).astype(jnp.int32)
    row_offs = entries[:, 3]
    col_offs = entries[:, 4]
    mask = hex_mask(SEG_PX)

    def cutout(segment_id, row_off, col_off, keep):
        piece = lax.dynamic_slice(segment_maps, (segment_id, row_off, col_off), (1, SUB, SUB))[0]
        shades = lax.dynamic_slice(mask, (row_off, col_off), (SUB, SUB)) * keep.astype(jnp.bfloat16)
        return (piece * shades, shades)
    patches, shades = jax.vmap(cutout)(segment_ids, row_offs, col_offs, usable)
    opd = jax.ops.segment_sum(patches.astype(jnp.float32), lens_ids, num_segments=LENSES)
    amplitude = jax.ops.segment_sum(shades.astype(jnp.float32), lens_ids, num_segments=LENSES)
    grad_opd = jnp.zeros((LENSES, SUB, SUB), jnp.float32)
    for wave_idx in range(NW):
        grad_opd = grad_opd + wave_grad(opd, amplitude, cotangent, wavelengths[wave_idx], NW)
    grad_patches = (grad_opd[lens_ids] * shades.astype(jnp.float32)).astype(jnp.bfloat16)
    offsets = jnp.arange(SUB, dtype=jnp.int32)
    rows = row_offs[:, None, None] + offsets[None, :, None]
    cols = col_offs[:, None, None] + offsets[None, None, :]
    segs = jnp.broadcast_to(segment_ids[:, None, None], rows.shape)
    rows = jnp.broadcast_to(rows, (count, SUB, SUB))
    cols = jnp.broadcast_to(cols, (count, SUB, SUB))
    totals = jnp.zeros((SEGMENTS, SEG_PX, SEG_PX), jnp.float32)
    return totals.at[segs, rows, cols].add(grad_patches.astype(jnp.float32))
```

```python
import functools
import math

import jax
import jax.numpy as jnp
from jax import lax
from jax.experimental import pallas as pl
from jax.experimental.pallas import tpu as pltpu
from jax.sharding import PartitionSpec as P

SUB = 64
LANES = 2 * SUB
HEAD = 16
WINDOW = SUB + 8
FIELDS = 5
SAMPLING = 0.5
GROUP = 2
UNROLL = 4
VMEM_LIMIT = 48 * 1024 * 1024

SINE = (4.442882919124343, -7.308245686509023, 3.6063542184319086, -0.8461116503677503, 0.10982451641387822)
COSINE = (1.4142134962552284, -6.978850948563799, 5.7394603769067665, -1.8835579059841794, 0.3106880275221932)


def horner(coefficients, z):
    total = coefficients[-1]
    for coefficient in coefficients[-2::-1]:
        total = total * z + coefficient
    return total


def half_turn(turns):
    r = turns - jnp.round(turns)
    z = r * r
    return horner(SINE, z) * r, horner(COSINE, z)


def row_limit(rows, first, extent):
    i = lax.broadcasted_iota(jnp.int32, (rows, LANES), 0) + first
    down = jnp.abs(2 * i - (extent - 1))
    return jnp.where(8 * down <= 7 * (extent - 1), 7 * (extent - 1) - 4 * down, -1)


def aligned(row, extent):
    base = pl.multiple_of(jnp.minimum(row // 8 * 8, extent - WINDOW), 8)
    return base, row - base


def sideways(first, extent):
    j = lax.broadcasted_iota(jnp.int32, (1, LANES), 1) + first
    return 7 * jnp.abs(2 * j - (extent - 1))


def cut_kernel(table, maps, out, masked):
    peers = out.shape[0]
    segs, extent, _ = maps.shape
    chunk = 32
    for row in range(0, extent, chunk):
        limit = row_limit(chunk, row, extent)
        for half in range(extent // LANES):
            inside = sideways(half * LANES, extent) <= limit
            for s in range(segs):
                spot = (s, pl.ds(row, chunk), pl.ds(half * LANES, LANES))
                masked[spot] = jnp.where(inside, maps[spot].astype(jnp.float32), 0.0)
    lane = lax.broadcasted_iota(jnp.int32, (SUB, LANES), 1)
    tall_lane = lax.broadcasted_iota(jnp.int32, (WINDOW, LANES), 1)
    head_lane = lax.broadcasted_iota(jnp.int32, (HEAD, LANES), 1)

    def one_peer(p, carry):
        head = jnp.zeros((HEAD, LANES), jnp.int32)
        sides = []
        for c in range(2):
            live, seg, row, col = (table[p, c, k] for k in (0, 1, 3, 4))
            base, down = aligned(row, extent)
            left = masked[seg, pl.ds(base, WINDOW), pl.ds(0, LANES)]
            right = masked[seg, pl.ds(base, WINDOW), pl.ds(LANES, LANES)]
            both = jnp.where(tall_lane >= col, left, right)
            both = pltpu.roll(both, jnp.where(down == 0, 0, WINDOW - down), axis=0)[:SUB]
            both = pltpu.roll(both, (2 * LANES + SUB * c - col) & (LANES - 1), axis=1)
            sides.append(both * live.astype(jnp.float32))
            for k in range(FIELDS):
                head = jnp.where(head_lane == FIELDS * c + k, table[p, c, k], head)
        out[p, pl.ds(0, SUB), :] = jnp.where(lane < SUB, sides[0], sides[1]).astype(jnp.bfloat16)
        out[p, pl.ds(SUB, HEAD), :] = head.astype(jnp.float32).astype(jnp.bfloat16)
        return carry

    lax.fori_loop(0, peers, one_peer, 0, unroll=2)


def wave_kernel(
    extent, waves_ref, message, cotangent, out,
    heads, table, place, slot_place, owner_of, opd, amplitude, grad, turns_per, left1, left2, right1, right2, sem,
):
    peers = message.shape[0]
    waves = waves_ref.shape[0]
    lenses, focal, _ = cotangent.shape
    pairs = opd.shape[0] - 1
    dead_place = 2 * pairs

    def one_head(p, carry):
        heads[pl.ds(p, 1), :] = message[p, pl.ds(SUB, HEAD), :].astype(jnp.float32)[0:1].astype(jnp.int32)
        return carry

    lax.fori_loop(0, peers, one_head, 0, unroll=4)
    copy = pltpu.make_async_copy(heads, table, sem)
    copy.start()

    opd[...] = jnp.zeros_like(opd)
    amplitude[...] = jnp.zeros_like(amplitude)

    position = lax.broadcasted_iota(jnp.int32, (focal, LANES), 0) - focal // 2
    lane = lax.broadcasted_iota(jnp.int32, (SUB, LANES), 1)
    across = lane % SUB - SUB // 2
    product = (position * across).astype(jnp.float32)
    lower = lane < SUB

    def one_table(w, carry):
        inverse = 1.0 / jnp.full((8, LANES), waves_ref[w], jnp.float32)
        turns_per[w] = inverse
        sine, cosine = half_turn(product * (-SAMPLING / SUB) * inverse[0:1])
        real = 1.0 - sine * sine
        imag = sine * cosine
        zero = jnp.zeros_like(real)
        left1[w, pl.ds(0, SUB), :] = jnp.where(lower, real, -imag).astype(jnp.bfloat16)
        left1[w, pl.ds(SUB, SUB), :] = jnp.where(lower, imag, real).astype(jnp.bfloat16)
        left2[w, pl.ds(0, SUB), :] = jnp.where(lower, real, imag).astype(jnp.bfloat16)
        left2[w, pl.ds(SUB, SUB), :] = jnp.where(lower, -imag, real).astype(jnp.bfloat16)
        for h in range(2):
            own = lower if h == 0 else ~lower
            re = jnp.where(own, real, zero).astype(jnp.bfloat16)
            im = jnp.where(own, imag, zero)
            minus = (-im).astype(jnp.bfloat16)
            im = im.astype(jnp.bfloat16)
            first = pl.ds(h * SUB, SUB)
            second = pl.ds(LANES + h * SUB, SUB)
            right1[w, first, pl.ds(0, LANES)] = re
            right1[w, first, pl.ds(LANES, LANES)] = im
            right1[w, second, pl.ds(0, LANES)] = minus
            right1[w, second, pl.ds(LANES, LANES)] = re
            right2[w, first, pl.ds(0, LANES)] = re
            right2[w, first, pl.ds(LANES, LANES)] = minus
            right2[w, second, pl.ds(0, LANES)] = im
            right2[w, second, pl.ds(LANES, LANES)] = re
        return carry

    lax.fori_loop(0, waves, one_table, 0)

    def clear(l, carry):
        place[l] = -1
        owner_of[l] = 0
        return carry

    lax.fori_loop(0, lenses, clear, 0)
    copy.wait()

    def one_slot(p, count):
        patch = message[p, pl.ds(0, SUB), :].astype(jnp.float32)
        for c in range(2):
            live = table[p, FIELDS * c] == 1
            lens, row, col = (table[p, FIELDS * c + k] for k in (2, 3, 4))
            before = place[lens]
            fresh = live & (before < 0)
            here = jnp.where(fresh, count, before)
            place[lens] = here
            owner_of[count] = jnp.where(fresh, lens, 0)
            count = count + fresh.astype(jnp.int32)
            here = jnp.where(live, here, dead_place)
            slot_place[2 * p + c] = here
            pair = here // 2
            half = here % 2
            own = lane // SUB == half
            moved = pltpu.roll(patch, SUB * jnp.where(half == c, 0, 1), axis=1)
            opd[pair] += jnp.where(own, moved, 0.0)
            inside = own & (sideways(col - SUB * half, extent) <= row_limit(SUB, row, extent))
            amplitude[pair] += jnp.where(inside, 1.0, 0.0)
        return count

    count = lax.fori_loop(0, peers, one_slot, 0)

    def one_group(g, carry):
        weights = []
        for i in range(GROUP):
            k = g * (2 * GROUP) + 2 * i
            pieces = [cotangent[owner_of[k + h]].astype(jnp.float32) for h in range(2)]
            weights.append(jnp.concatenate(pieces, axis=1) * (2.0 / (waves * SUB)))
            grad[g * GROUP + i] = jnp.zeros((SUB, LANES), jnp.float32)

        def one_wave(w):
            scale = turns_per[w][0:1]
            reals, imags = [], []
            for i in range(GROUP):
                amp = amplitude[g * GROUP + i]
                sine, cosine = half_turn(opd[g * GROUP + i] * scale)
                part = amp * sine
                reals.append(amp - part * sine)
                imags.append(part * cosine)

            def stack(res, ims):
                top = jnp.concatenate([x.astype(jnp.bfloat16) for x in res], axis=1)
                low = jnp.concatenate([x.astype(jnp.bfloat16) for x in ims], axis=1)
                return jnp.concatenate([top, low], axis=0)

            def line(x):
                x = x.astype(jnp.bfloat16)
                rows = []
                for i in range(GROUP):
                    at = slice(LANES * i, LANES * (i + 1))
                    rows.append(jnp.concatenate([x[:SUB, at], x[SUB:, at]], axis=1))
                return jnp.concatenate(rows, axis=0)

            p = jnp.dot(left1[w], stack(reals, imags), preferred_element_type=jnp.float32)
            f = jnp.dot(line(p), right1[w], preferred_element_type=jnp.float32)
            held = [[], []]
            for i in range(GROUP):
                for h in range(2):
                    held[h].append(f[SUB * i : SUB * (i + 1), LANES * h : LANES * (h + 1)] * weights[i])
            q = jnp.dot(left2[w], stack(*held), preferred_element_type=jnp.float32)
            b = jnp.dot(line(q), right2[w], preferred_element_type=jnp.float32)
            factor = scale * (2.0 * math.pi / SUB)
            for i in range(GROUP):
                back = b[SUB * i : SUB * (i + 1)]
                grad[g * GROUP + i] += factor * (reals[i] * back[:, LANES:] - imags[i] * back[:, :LANES])

        def some_waves(step, inner):
            for u in range(UNROLL):
                one_wave(step * UNROLL + u)
            return inner

        lax.fori_loop(0, waves // UNROLL, some_waves, 0)
        return carry

    lax.fori_loop(0, (count + 2 * GROUP - 1) // (2 * GROUP), one_group, 0)

    def one_return(p, carry):
        sides = []
        for c in range(2):
            here = slot_place[2 * p + c]
            row, col = table[p, FIELDS * c + 3], table[p, FIELDS * c + 4]
            pair = here // 2
            half = here % 2
            moved = pltpu.roll(grad[pair], SUB * jnp.where(half == c, 0, 1), axis=1)
            reach = jnp.where(here < dead_place, row_limit(SUB, row, extent), -1)
            sides.append(jnp.where(sideways(col - SUB * c, extent) <= reach, moved, 0.0))
        out[p] = jnp.where(lower, sides[0], sides[1]).astype(jnp.bfloat16)
        return carry

    lax.fori_loop(0, peers, one_return, 0, unroll=2)


def place_kernel(table, patches, out):
    peers = patches.shape[0]
    extent = out.shape[1]
    lane = lax.broadcasted_iota(jnp.int32, (WINDOW, LANES), 1)
    spare = jnp.zeros((WINDOW - SUB, LANES), jnp.float32)
    out[...] = jnp.zeros_like(out)

    def one_peer(p, carry):
        both = jnp.concatenate([patches[p].astype(jnp.float32), spare], axis=0)
        for c in range(2):
            seg, row, col = (table[p, c, k] for k in (1, 3, 4))
            base, down = aligned(row, extent)
            moved = pltpu.roll(both, (col + LANES - SUB * c) & (LANES - 1), axis=1)
            moved = pltpu.roll(moved, down, axis=0)
            for half in range(2):
                j = lane + (half * LANES - col)
                kept = jnp.where((j >= 0) & (j < SUB), moved, 0.0)
                spot = (seg, pl.ds(base, WINDOW), pl.ds(half * LANES, LANES))
                out[spot] += kept
        return carry

    lax.fori_loop(0, peers, one_peer, 0)


def on_device(segment_maps, cotangent, wavelengths, intersections):
    peers = intersections.shape[0]
    waves = wavelengths.shape[0]
    lenses = cotangent.shape[0]
    segs, extent, _ = segment_maps.shape
    pairs = -(-lenses // (2 * GROUP)) * GROUP
    vmem = pl.BlockSpec(memory_space=pltpu.VMEM)
    smem = pl.BlockSpec(memory_space=pltpu.SMEM)
    params = pltpu.CompilerParams(vmem_limit_bytes=VMEM_LIMIT)

    message = pl.pallas_call(
        cut_kernel,
        out_shape=jax.ShapeDtypeStruct((peers, SUB + HEAD, LANES), jnp.bfloat16),
        in_specs=[smem, vmem],
        out_specs=vmem,
        scratch_shapes=[pltpu.VMEM((segs, extent, extent), jnp.float32)],
        compiler_params=params,
        name="cut_patches",
    )(intersections, segment_maps)
    arriving = lax.all_to_all(message, "tile", split_axis=0, concat_axis=0, tiled=True)
    grads = pl.pallas_call(
        functools.partial(wave_kernel, extent),
        out_shape=jax.ShapeDtypeStruct((peers, SUB, LANES), jnp.bfloat16),
        in_specs=[smem, vmem, vmem],
        out_specs=vmem,
        scratch_shapes=[
            pltpu.VMEM((peers, LANES), jnp.int32),
            pltpu.SMEM((peers, LANES), jnp.int32),
            pltpu.SMEM((lenses,), jnp.int32),
            pltpu.SMEM((2 * peers,), jnp.int32),
            pltpu.SMEM((2 * pairs + 1,), jnp.int32),
            pltpu.VMEM((pairs + 1, SUB, LANES), jnp.float32),
            pltpu.VMEM((pairs + 1, SUB, LANES), jnp.float32),
            pltpu.VMEM((pairs + 1, SUB, LANES), jnp.float32),
            pltpu.VMEM((waves, 8, LANES), jnp.float32),
            pltpu.VMEM((waves, LANES, LANES), jnp.bfloat16),
            pltpu.VMEM((waves, LANES, LANES), jnp.bfloat16),
            pltpu.VMEM((waves, 2 * LANES, 2 * LANES), jnp.bfloat16),
            pltpu.VMEM((waves, 2 * LANES, 2 * LANES), jnp.bfloat16),
            pltpu.SemaphoreType.DMA,
        ],
        compiler_params=params,
        name="wave_gradients",
    )(wavelengths, arriving, cotangent)
    returned = lax.all_to_all(grads, "tile", split_axis=0, concat_axis=0, tiled=True)
    return pl.pallas_call(
        place_kernel,
        out_shape=jax.ShapeDtypeStruct((segs, extent, extent), jnp.float32),
        in_specs=[smem, vmem],
        out_specs=vmem,
        compiler_params=params,
        name="place_gradients",
    )(intersections, returned)


def solution(mesh):
    return jax.shard_map(
        on_device,
        mesh=mesh,
        in_specs=(
            P(("case", "tile"), None, None),
            P(("case", "tile"), None, None),
            P(),
            P(("case", "tile"), None, None),
        ),
        out_specs=P(("case", "tile"), None, None),
        check_vma=False,
    )
```

```python
import functools
import math

import jax
import jax.numpy as jnp
from jax import lax
from jax.experimental import pallas as pl
from jax.experimental.pallas import tpu as pltpu
from jax.sharding import PartitionSpec as P

SUB = 64
LANES = 2 * SUB
HEAD = 8
WINDOW = SUB + 8
FIELDS = 5
SAMPLING = 0.5
GROUP = 4
UNROLL = 16
ORDER = (0, 1, 2, 3, 4)
VMEM_LIMIT = 48 * 1024 * 1024

SINE = (4.442882919124343, -7.308245686509023, 3.6063542184319086, -0.8461116503677503, 0.10982451641387822)
COSINE = (1.4142134962552284, -6.978850948563799, 5.7394603769067665, -1.8835579059841794, 0.3106880275221932)


def horner(coefficients, z):
    total = coefficients[-1]
    for coefficient in coefficients[-2::-1]:
        total = total * z + coefficient
    return total


def half_turn(turns):
    r = turns - jnp.round(turns)
    z = r * r
    return horner(SINE, z) * r, horner(COSINE, z)


def row_limit(rows, first, extent):
    i = lax.broadcasted_iota(jnp.int32, (rows, LANES), 0) + first
    down = jnp.abs(2 * i - (extent - 1))
    return jnp.where(8 * down <= 7 * (extent - 1), 7 * (extent - 1) - 4 * down, -1)


def aligned(row, extent):
    base = pl.multiple_of(jnp.minimum(row // 8 * 8, extent - WINDOW), 8)
    return base, row - base


def sideways(first, extent):
    j = lax.broadcasted_iota(jnp.int32, (1, LANES), 1) + first
    return 7 * jnp.abs(2 * j - (extent - 1))


def cut_kernel(table, maps, out, masked):
    peers = out.shape[0]
    segs, extent, _ = maps.shape
    chunk = 32
    for row in range(0, extent, chunk):
        limit = row_limit(chunk, row, extent)
        for half in range(extent // LANES):
            inside = sideways(half * LANES, extent) <= limit
            for s in range(segs):
                spot = (s, pl.ds(row, chunk), pl.ds(half * LANES, LANES))
                masked[spot] = jnp.where(inside, maps[spot].astype(jnp.float32), 0.0)
    lane = lax.broadcasted_iota(jnp.int32, (SUB, LANES), 1)
    tall_lane = lax.broadcasted_iota(jnp.int32, (WINDOW, LANES), 1)
    head_lane = lax.broadcasted_iota(jnp.int32, (HEAD, LANES), 1)

    def one_peer(p, carry):
        head = jnp.zeros((HEAD, LANES), jnp.int32)
        sides = []
        for c in range(2):
            live, seg, row, col = (table[p, c, k] for k in (0, 1, 3, 4))
            base, down = aligned(row, extent)
            left = masked[seg, pl.ds(base, WINDOW), pl.ds(0, LANES)]
            right = masked[seg, pl.ds(base, WINDOW), pl.ds(LANES, LANES)]
            both = jnp.where(tall_lane >= col, left, right)
            both = pltpu.roll(both, jnp.where(down == 0, 0, WINDOW - down), axis=0)[:SUB]
            both = pltpu.roll(both, (2 * LANES + SUB * c - col) & (LANES - 1), axis=1)
            sides.append(both * live.astype(jnp.float32))
            for k in range(FIELDS):
                head = jnp.where(head_lane == FIELDS * c + k, table[p, c, k], head)
        out[p, pl.ds(0, SUB), :] = jnp.where(lane < SUB, sides[0], sides[1]).astype(jnp.bfloat16)
        out[p, pl.ds(SUB, HEAD), :] = head.astype(jnp.float32).astype(jnp.bfloat16)
        return carry

    lax.fori_loop(0, peers, one_peer, 0, unroll=2)


def wave_kernel(
    extent, waves_ref, message, cotangent, out,
    heads, table, place, slot_place, owner_of, opd, amplitude, grad, turns_per, left1, left2, right1, right2, sem,
):
    peers = message.shape[0]
    waves = waves_ref.shape[0]
    lenses, focal, _ = cotangent.shape
    pairs = opd.shape[0] - 1
    dead_place = 2 * pairs

    def one_head(p, carry):
        heads[pl.ds(p, 1), :] = message[p, pl.ds(SUB, HEAD), :].astype(jnp.float32)[0:1].astype(jnp.int32)
        return carry

    lax.fori_loop(0, peers, one_head, 0, unroll=4)
    copy = pltpu.make_async_copy(heads, table, sem)
    copy.start()

    opd[...] = jnp.zeros_like(opd)
    amplitude[...] = jnp.zeros_like(amplitude)

    position = lax.broadcasted_iota(jnp.int32, (focal, LANES), 0) - focal // 2
    lane = lax.broadcasted_iota(jnp.int32, (SUB, LANES), 1)
    across = lane % SUB - SUB // 2
    product = (position * across).astype(jnp.float32)
    lower = lane < SUB

    def one_table(w, carry):
        inverse = 1.0 / jnp.full((8, LANES), waves_ref[w], jnp.float32)
        turns_per[w] = inverse
        sine, cosine = half_turn(product * (-SAMPLING / SUB) * inverse[0:1])
        real = 1.0 - sine * sine
        imag = sine * cosine
        zero = jnp.zeros_like(real)
        left1[w, pl.ds(0, SUB), :] = jnp.where(lower, real, -imag).astype(jnp.bfloat16)
        left1[w, pl.ds(SUB, SUB), :] = jnp.where(lower, imag, real).astype(jnp.bfloat16)
        left2[w, pl.ds(0, SUB), :] = jnp.where(lower, real, imag).astype(jnp.bfloat16)
        left2[w, pl.ds(SUB, SUB), :] = jnp.where(lower, -imag, real).astype(jnp.bfloat16)
        for h in range(2):
            own = lower if h == 0 else ~lower
            re = jnp.where(own, real, zero).astype(jnp.bfloat16)
            im = jnp.where(own, imag, zero)
            minus = (-im).astype(jnp.bfloat16)
            im = im.astype(jnp.bfloat16)
            first = pl.ds(h * SUB, SUB)
            second = pl.ds(LANES + h * SUB, SUB)
            right1[w, first, pl.ds(0, LANES)] = re
            right1[w, first, pl.ds(LANES, LANES)] = im
            right1[w, second, pl.ds(0, LANES)] = minus
            right1[w, second, pl.ds(LANES, LANES)] = re
            right2[w, first, pl.ds(0, LANES)] = re
            right2[w, first, pl.ds(LANES, LANES)] = minus
            right2[w, second, pl.ds(0, LANES)] = im
            right2[w, second, pl.ds(LANES, LANES)] = re
        return carry

    lax.fori_loop(0, waves, one_table, 0)

    def clear(l, carry):
        place[l] = -1
        owner_of[l] = 0
        return carry

    lax.fori_loop(0, lenses, clear, 0)
    copy.wait()

    def one_slot(p, count):
        patch = message[p, pl.ds(0, SUB), :].astype(jnp.float32)
        for c in range(2):
            live = table[p, FIELDS * c] == 1
            lens, row, col = (table[p, FIELDS * c + k] for k in (2, 3, 4))
            before = place[lens]
            fresh = live & (before < 0)
            here = jnp.where(fresh, count, before)
            place[lens] = here
            owner_of[count] = jnp.where(fresh, lens, 0)
            count = count + fresh.astype(jnp.int32)
            here = jnp.where(live, here, dead_place)
            slot_place[2 * p + c] = here
            pair = here // 2
            half = here % 2
            own = lane // SUB == half
            moved = pltpu.roll(patch, SUB * jnp.where(half == c, 0, 1), axis=1)
            opd[pair] += jnp.where(own, moved, 0.0)
            inside = own & (sideways(col - SUB * half, extent) <= row_limit(SUB, row, extent))
            amplitude[pair] += jnp.where(inside, 1.0, 0.0)
        return count

    count = lax.fori_loop(0, peers, one_slot, 0)

    def one_group(g, carry):
        weights = []
        for i in range(GROUP):
            k = g * (2 * GROUP) + 2 * i
            pieces = [cotangent[owner_of[k + h]].astype(jnp.float32) for h in range(2)]
            weights.append(jnp.concatenate(pieces, axis=1) * (2.0 / (waves * SUB)))
            grad[g * GROUP + i] = jnp.zeros((SUB, LANES), jnp.float32)

        def stack(res, ims):
            top = jnp.concatenate([x.astype(jnp.bfloat16) for x in res], axis=1)
            low = jnp.concatenate([x.astype(jnp.bfloat16) for x in ims], axis=1)
            return jnp.concatenate([top, low], axis=0)

        def line(x):
            x = x.astype(jnp.bfloat16)
            rows = []
            for i in range(GROUP):
                at = slice(LANES * i, LANES * (i + 1))
                rows.append(jnp.concatenate([x[:SUB, at], x[SUB:, at]], axis=1))
            return jnp.concatenate(rows, axis=0)

        def field(w):
            scale = turns_per[w][0:1]
            reals, imags = [], []
            for i in range(GROUP):
                amp = amplitude[g * GROUP + i]
                sine, cosine = half_turn(opd[g * GROUP + i] * scale)
                part = amp * sine
                reals.append(amp - part * sine)
                imags.append(part * cosine)
            return reals, imags, stack(reals, imags)

        def pupil_rows(w, state):
            reals, imags, e = state
            return reals, imags, line(jnp.dot(left1[w], e, preferred_element_type=jnp.float32))

        def pupil_columns(w, state):
            reals, imags, p = state
            f = jnp.dot(p, right1[w], preferred_element_type=jnp.float32)
            held = [[], []]
            for i in range(GROUP):
                for h in range(2):
                    held[h].append(f[SUB * i : SUB * (i + 1), LANES * h : LANES * (h + 1)] * weights[i])
            return reals, imags, stack(*held)

        def focal_rows(w, state):
            reals, imags, held = state
            return reals, imags, line(jnp.dot(left2[w], held, preferred_element_type=jnp.float32))

        def focal_columns(w, state):
            reals, imags, q = state
            b = jnp.dot(q, right2[w], preferred_element_type=jnp.float32)
            factor = turns_per[w][0:1] * (2.0 * math.pi / SUB)
            for i in range(GROUP):
                back = b[SUB * i : SUB * (i + 1)]
                grad[g * GROUP + i] += factor * (reals[i] * back[:, LANES:] - imags[i] * back[:, :LANES])

        def some_waves(step, inner):
            stages = (pupil_rows, pupil_columns, focal_rows, focal_columns)
            states = {}
            for t in range(UNROLL + len(stages)):
                for k in ORDER:
                    u = t - k
                    if 0 <= u < UNROLL:
                        w = step * UNROLL + u
                        states[u] = field(w) if k == 0 else stages[k - 1](w, states[u])
            return inner

        lax.fori_loop(0, waves // UNROLL, some_waves, 0)
        return carry

    lax.fori_loop(0, (count + 2 * GROUP - 1) // (2 * GROUP), one_group, 0)

    def one_return(p, carry):
        sides = []
        for c in range(2):
            here = slot_place[2 * p + c]
            row, col = table[p, FIELDS * c + 3], table[p, FIELDS * c + 4]
            pair = here // 2
            half = here % 2
            moved = pltpu.roll(grad[pair], SUB * jnp.where(half == c, 0, 1), axis=1)
            reach = jnp.where(here < dead_place, row_limit(SUB, row, extent), -1)
            sides.append(jnp.where(sideways(col - SUB * c, extent) <= reach, moved, 0.0))
        out[p] = jnp.where(lower, sides[0], sides[1]).astype(jnp.bfloat16)
        return carry

    lax.fori_loop(0, peers, one_return, 0, unroll=2)


def wave_call(wavelengths, message, cotangent, extent):
    peers = message.shape[0]
    waves = wavelengths.shape[0]
    lenses = cotangent.shape[0]
    pairs = -(-lenses // (2 * GROUP)) * GROUP
    vmem = pl.BlockSpec(memory_space=pltpu.VMEM)
    smem = pl.BlockSpec(memory_space=pltpu.SMEM)
    return pl.pallas_call(
        functools.partial(wave_kernel, extent),
        out_shape=jax.ShapeDtypeStruct((peers, SUB, LANES), jnp.bfloat16),
        in_specs=[smem, vmem, vmem],
        out_specs=vmem,
        scratch_shapes=[
            pltpu.VMEM((peers, LANES), jnp.int32),
            pltpu.SMEM((peers, LANES), jnp.int32),
            pltpu.SMEM((lenses,), jnp.int32),
            pltpu.SMEM((2 * peers,), jnp.int32),
            pltpu.SMEM((2 * pairs + 1,), jnp.int32),
            pltpu.VMEM((pairs + 1, SUB, LANES), jnp.float32),
            pltpu.VMEM((pairs + 1, SUB, LANES), jnp.float32),
            pltpu.VMEM((pairs + 1, SUB, LANES), jnp.float32),
            pltpu.VMEM((waves, 8, LANES), jnp.float32),
            pltpu.VMEM((waves, LANES, LANES), jnp.bfloat16),
            pltpu.VMEM((waves, LANES, LANES), jnp.bfloat16),
            pltpu.VMEM((waves, 2 * LANES, 2 * LANES), jnp.bfloat16),
            pltpu.VMEM((waves, 2 * LANES, 2 * LANES), jnp.bfloat16),
            pltpu.SemaphoreType.DMA,
        ],
        compiler_params=pltpu.CompilerParams(vmem_limit_bytes=VMEM_LIMIT),
        name="wave_gradients",
    )(wavelengths, message, cotangent)


def place_kernel(table, patches, out):
    peers = patches.shape[0]
    extent = out.shape[1]
    lane = lax.broadcasted_iota(jnp.int32, (WINDOW, LANES), 1)
    spare = jnp.zeros((WINDOW - SUB, LANES), jnp.float32)
    out[...] = jnp.zeros_like(out)

    def one_peer(p, carry):
        both = jnp.concatenate([patches[p].astype(jnp.float32), spare], axis=0)
        for c in range(2):
            seg, row, col = (table[p, c, k] for k in (1, 3, 4))
            base, down = aligned(row, extent)
            moved = pltpu.roll(both, (col + LANES - SUB * c) & (LANES - 1), axis=1)
            moved = pltpu.roll(moved, down, axis=0)
            for half in range(2):
                j = lane + (half * LANES - col)
                kept = jnp.where((j >= 0) & (j < SUB), moved, 0.0)
                spot = (seg, pl.ds(base, WINDOW), pl.ds(half * LANES, LANES))
                out[spot] += kept
        return carry

    lax.fori_loop(0, peers, one_peer, 0)


def on_device(segment_maps, cotangent, wavelengths, intersections):
    peers = intersections.shape[0]
    segs, extent, _ = segment_maps.shape
    vmem = pl.BlockSpec(memory_space=pltpu.VMEM)
    smem = pl.BlockSpec(memory_space=pltpu.SMEM)
    params = pltpu.CompilerParams(vmem_limit_bytes=VMEM_LIMIT)

    message = pl.pallas_call(
        cut_kernel,
        out_shape=jax.ShapeDtypeStruct((peers, SUB + HEAD, LANES), jnp.bfloat16),
        in_specs=[smem, vmem],
        out_specs=vmem,
        scratch_shapes=[pltpu.VMEM((segs, extent, extent), jnp.float32)],
        compiler_params=params,
        name="cut_patches",
    )(intersections, segment_maps)
    arriving = lax.all_to_all(message, "tile", split_axis=0, concat_axis=0, tiled=True)
    grads = wave_call(wavelengths, arriving, cotangent, extent)
    returned = lax.all_to_all(grads, "tile", split_axis=0, concat_axis=0, tiled=True)
    return pl.pallas_call(
        place_kernel,
        out_shape=jax.ShapeDtypeStruct((segs, extent, extent), jnp.float32),
        in_specs=[smem, vmem],
        out_specs=vmem,
        compiler_params=params,
        name="place_gradients",
    )(intersections, returned)


def solution(mesh):
    return jax.shard_map(
        on_device,
        mesh=mesh,
        in_specs=(
            P(("case", "tile"), None, None),
            P(("case", "tile"), None, None),
            P(),
            P(("case", "tile"), None, None),
        ),
        out_specs=P(("case", "tile"), None, None),
        check_vma=False,
    )
```

```python
import functools
import math

import jax
import jax.numpy as jnp
from jax import lax
from jax.experimental import pallas as pl
from jax.experimental.pallas import tpu as pltpu
from jax.sharding import PartitionSpec as P

SUB = 64
LANES = 2 * SUB
HEAD = 8
WINDOW = SUB + 8
FIELDS = 5
SAMPLING = 0.5
GROUP = 4
GROUP_FEW = 5
FEW = 20
VMEM_LIMIT = 48 * 1024 * 1024

LEAD = -0.7843722149521581
SINE = tuple(a / LEAD for a in (4.442867901299065, -7.307443351304121, 3.594787401596918))
COSINE = tuple(a / LEAD for a in (1.4142040792740376, -6.9776419299271595, 5.715236658714806, -1.7283430271755356))


FINE_SINE = (4.442882834139933, -7.308241153900929, 3.6062889473067714, -0.8457635292158341, 0.10920561913977103)
FINE_COSINE = (1.4142134965588182, -6.978850987079529, 5.739461141869117, -1.8835627683436942, 0.3106976855933321)


def horner(coefficients, z):
    total = coefficients[-1]
    for coefficient in coefficients[-2::-1]:
        total = total * z + coefficient
    return total


def half_turn(turns):
    r = turns - jnp.round(turns)
    z = r * r
    sine = (((z + SINE[2]) * z + SINE[1]) * z + SINE[0]) * r
    cosine = ((COSINE[3] * z + COSINE[2]) * z + COSINE[1]) * z + COSINE[0]
    return sine, cosine


def row_limit(rows, first, extent):
    i = lax.broadcasted_iota(jnp.int32, (rows, LANES), 0) + first
    down = jnp.abs(2 * i - (extent - 1))
    return jnp.where(8 * down <= 7 * (extent - 1), 7 * (extent - 1) - 4 * down, -1)


def aligned(row, extent):
    base = pl.multiple_of(jnp.minimum(row // 8 * 8, extent - WINDOW), 8)
    return base, row - base


def sideways(first, extent):
    j = lax.broadcasted_iota(jnp.int32, (1, LANES), 1) + first
    return 7 * jnp.abs(2 * j - (extent - 1))


def window(image, row, col, extent, side):
    base, down = aligned(row, extent)
    left = image[pl.ds(base, WINDOW), pl.ds(0, LANES)]
    right = image[pl.ds(base, WINDOW), pl.ds(LANES, LANES)]
    lane = lax.broadcasted_iota(jnp.int32, (WINDOW, LANES), 1)
    both = jnp.where(lane >= col, left, right)
    both = pltpu.roll(both, jnp.where(down == 0, 0, WINDOW - down), axis=0)[:SUB]
    return pltpu.roll(both, (2 * LANES + SUB * side - col) & (LANES - 1), axis=1)


def fill_mask(mask):
    extent = mask.shape[0]
    chunk = 32
    for row in range(0, extent, chunk):
        limit = row_limit(chunk, row, extent)
        for half in range(extent // LANES):
            inside = sideways(half * LANES, extent) <= limit
            mask[pl.ds(row, chunk), pl.ds(half * LANES, LANES)] = jnp.where(inside, 1.0, 0.0)


def read_table(entries, heads, table, sem):
    for p in range(entries.shape[0]):
        heads[pl.ds(2 * p, 2), pl.ds(0, FIELDS)] = entries[p]
    copy = pltpu.make_async_copy(heads, table, sem)
    copy.start()
    return copy


def cut_kernel(entries, maps, out, heads, table, raw, masked, sem, map_sems):
    peers = out.shape[0]
    segs, extent, _ = maps.shape
    loads = [pltpu.make_async_copy(maps.at[s], raw.at[s], map_sems.at[s]) for s in range(segs)]
    for load in loads:
        load.start()
    copy = read_table(entries, heads, table, sem)
    lower = lax.broadcasted_iota(jnp.int32, (SUB, LANES), 1) < SUB
    for p in range(peers):
        out[p, pl.ds(SUB, HEAD), :] = jnp.zeros((HEAD, LANES), jnp.bfloat16)
        out[p, pl.ds(SUB, 2), pl.ds(0, FIELDS)] = entries[p].astype(jnp.float32).astype(jnp.bfloat16)
    chunk = 32
    for s in range(segs):
        loads[s].wait()
        for row in range(0, extent, chunk):
            limit = row_limit(chunk, row, extent)
            for half in range(extent // LANES):
                inside = sideways(half * LANES, extent) <= limit
                spot = (s, pl.ds(row, chunk), pl.ds(half * LANES, LANES))
                masked[spot] = jnp.where(inside, raw[spot].astype(jnp.float32), 0.0)
    copy.wait()

    def one_peer(p, carry):
        sides = []
        for c in range(2):
            live, seg, row, col = (table[2 * p + c, k] for k in (0, 1, 3, 4))
            piece = window(masked.at[seg], row, col, extent, c)
            sides.append(piece * live.astype(jnp.float32))
        out[p, pl.ds(0, SUB), :] = jnp.where(lower, sides[0], sides[1]).astype(jnp.bfloat16)
        return carry

    lax.fori_loop(0, peers, one_peer, 0, unroll=8)


def table_kernel(waves_ref, turns_per, left1, left2, right1, right2):
    waves = waves_ref.shape[0]
    position = lax.broadcasted_iota(jnp.int32, (SUB, LANES), 0) - SUB // 2
    lane = lax.broadcasted_iota(jnp.int32, (SUB, LANES), 1)
    across = (lane & (SUB - 1)) - SUB // 2
    product = (position * across).astype(jnp.float32) * (-SAMPLING / SUB)
    lower = lane < SUB

    def one_table(w, carry):
        inverse = 1.0 / jnp.full((8, LANES), waves_ref[w], jnp.float32)
        turns_per[w] = inverse
        turns = product * inverse[0:1]
        r = turns - jnp.round(turns)
        z = r * r
        sine = horner(FINE_SINE, z) * r
        real = 1.0 - sine * sine
        imag = sine * horner(FINE_COSINE, z)
        zero = jnp.zeros_like(real)
        left1[w, pl.ds(0, SUB), :] = jnp.where(lower, real, -imag).astype(jnp.bfloat16)
        left1[w, pl.ds(SUB, SUB), :] = jnp.where(lower, imag, real).astype(jnp.bfloat16)
        left2[w, pl.ds(0, SUB), :] = jnp.where(lower, real, imag).astype(jnp.bfloat16)
        left2[w, pl.ds(SUB, SUB), :] = jnp.where(lower, -imag, real).astype(jnp.bfloat16)
        for h in range(2):
            own = lower if h == 0 else ~lower
            re = jnp.where(own, real, zero).astype(jnp.bfloat16)
            im = jnp.where(own, imag, zero)
            minus = (-im).astype(jnp.bfloat16)
            im = im.astype(jnp.bfloat16)
            first = pl.ds(h * SUB, SUB)
            second = pl.ds(LANES + h * SUB, SUB)
            right1[w, first, pl.ds(0, LANES)] = re
            right1[w, first, pl.ds(LANES, LANES)] = im
            right1[w, second, pl.ds(0, LANES)] = minus
            right1[w, second, pl.ds(LANES, LANES)] = re
            right2[w, first, pl.ds(0, LANES)] = re
            right2[w, first, pl.ds(LANES, LANES)] = minus
            right2[w, second, pl.ds(0, LANES)] = im
            right2[w, second, pl.ds(LANES, LANES)] = re
        return carry

    lax.fori_loop(0, waves, one_table, 0)


def table_call(wavelengths):
    waves = wavelengths.shape[0]
    vmem = pl.BlockSpec(memory_space=pltpu.VMEM)
    return pl.pallas_call(
        table_kernel,
        out_shape=[
            jax.ShapeDtypeStruct((waves, 8, LANES), jnp.float32),
            jax.ShapeDtypeStruct((waves, LANES, LANES), jnp.bfloat16),
            jax.ShapeDtypeStruct((waves, LANES, LANES), jnp.bfloat16),
            jax.ShapeDtypeStruct((waves, 2 * LANES, 2 * LANES), jnp.bfloat16),
            jax.ShapeDtypeStruct((waves, 2 * LANES, 2 * LANES), jnp.bfloat16),
        ],
        in_specs=[pl.BlockSpec(memory_space=pltpu.SMEM)],
        out_specs=[vmem] * 5,
        compiler_params=pltpu.CompilerParams(vmem_limit_bytes=VMEM_LIMIT),
        cost_estimate=pl.CostEstimate(flops=10_000_000, bytes_accessed=6_000_000, transcendentals=0),
        name="lens_tables",
    )(wavelengths)


def wave_groups(group, count, owner_of, cotangent, opd, amplitude, grad, turns_per, left1, left2, right1, right2):
    waves = turns_per.shape[0]

    def stack(res, ims):
        top = jnp.concatenate([x.astype(jnp.bfloat16) for x in res], axis=1)
        low = jnp.concatenate([x.astype(jnp.bfloat16) for x in ims], axis=1)
        return jnp.concatenate([top, low], axis=0)

    def line(x):
        x = x.astype(jnp.bfloat16)
        rows = []
        for i in range(group):
            at = slice(LANES * i, LANES * (i + 1))
            rows.append(jnp.concatenate([x[:SUB, at], x[SUB:, at]], axis=1))
        return jnp.concatenate(rows, axis=0)

    def one_group(g, carry):
        weights, scaled = [], []
        totals = [None] * group
        for i in range(group):
            k = (g * group + i) * 2
            pieces = [cotangent[owner_of[k + h]].astype(jnp.float32) for h in range(2)]
            scaled.append(amplitude[g * group + i] * LEAD**2)
            weights.append(jnp.concatenate(pieces, axis=1) * (2.0 / (waves * SUB)))

        def field(w, state):
            scale = turns_per[w][0:1]
            reals, imags = [], []
            for i in range(group):
                sine, cosine = half_turn(opd[g * group + i] * scale)
                part = scaled[i] * sine
                reals.append(amplitude[g * group + i] - part * sine)
                imags.append(part * cosine)
            return reals, imags, stack(reals, imags)

        def pupil_rows(w, state):
            reals, imags, e = state
            return reals, imags, line(jnp.dot(left1[w], e, preferred_element_type=jnp.float32))

        def pupil_columns(w, state):
            reals, imags, p = state
            f = jnp.dot(p, right1[w], preferred_element_type=jnp.float32)
            held = [[], []]
            for i in range(group):
                for h in range(2):
                    held[h].append(f[SUB * i : SUB * (i + 1), LANES * h : LANES * (h + 1)] * weights[i])
            return reals, imags, stack(*held)

        def focal_rows(w, state):
            reals, imags, held = state
            return reals, imags, line(jnp.dot(left2[w], held, preferred_element_type=jnp.float32))

        def focal_columns(w, state):
            reals, imags, q = state
            b = jnp.dot(q, right2[w], preferred_element_type=jnp.float32)
            factor = turns_per[w][0:1] * (2.0 * math.pi / SUB)
            for i in range(group):
                back = b[SUB * i : SUB * (i + 1)]
                term = factor * (reals[i] * back[:, LANES:] - imags[i] * back[:, :LANES])
                totals[i] = term if totals[i] is None else totals[i] + term

        stages = (field, pupil_rows, pupil_columns, focal_rows, focal_columns)
        states = [None] * waves
        for t in range(waves + len(stages) - 1):
            for k, stage in enumerate(stages):
                if 0 <= t - k < waves:
                    states[t - k] = stage(t - k, states[t - k])
        for i in range(group):
            grad[g * group + i] = totals[i]
        return carry

    lax.fori_loop(0, (count + 2 * group - 1) // (2 * group), one_group, 0)


def wave_kernel(
    message, cotangent, turns_far, left1_far, left2_far, right1_far, right2_far, out,
    turns_per, left1, left2, right1, right2,
    heads, table, place, slot_place, owner_of, opd, amplitude, grad, shades, mask, sem, table_sems,
):
    peers = message.shape[0]
    lenses = cotangent.shape[0]
    pairs = opd.shape[0] - 1
    extent = mask.shape[0]
    dead_place = 2 * pairs

    far = (turns_far, left1_far, right1_far, left2_far, right2_far)
    near = (turns_per, left1, right1, left2, right2)
    loads = [pltpu.make_async_copy(x, y, table_sems.at[i]) for i, (x, y) in enumerate(zip(far, near))]
    for load in loads:
        load.start()
    for p in range(peers):
        head = message[p, pl.ds(SUB, HEAD), :].astype(jnp.float32)[0:2]
        heads[pl.ds(2 * p, 2), :] = head.astype(jnp.int32)
    copy = pltpu.make_async_copy(heads, table, sem)
    copy.start()
    fill_mask(mask)
    opd[...] = jnp.zeros_like(opd)
    amplitude[...] = jnp.zeros_like(amplitude)
    lane = lax.broadcasted_iota(jnp.int32, (SUB, LANES), 1)
    lower = lane < SUB
    for l in range(lenses):
        place[l] = -1
    for k in range(dead_place + 1):
        owner_of[k] = 0
    copy.wait()

    def one_place(i, count):
        live = table[i, 0] == 1
        lens = table[i, 2]
        before = place[lens]
        fresh = live & (before < 0)
        here = jnp.where(fresh, count, before)
        place[lens] = here
        owner_of[count] = jnp.where(fresh, lens, 0)
        slot_place[i] = jnp.where(live, here, dead_place)
        return count + fresh.astype(jnp.int32)

    count = lax.fori_loop(0, 2 * peers, one_place, 0, unroll=4)

    def one_slot(p, carry):
        patch = message[p, pl.ds(0, SUB), :].astype(jnp.float32)
        sides = []
        for c in range(2):
            live, row, col = (table[2 * p + c, k] for k in (0, 3, 4))
            sides.append(window(mask, row, col, extent, c) * live.astype(jnp.float32))
        shade = jnp.where(lower, sides[0], sides[1])
        shades[p] = shade
        for c in range(2):
            here = slot_place[2 * p + c]
            pair = here >> 1
            half = here & 1
            turn = (half ^ c) * SUB
            own = (lane >> 6) == half
            opd[pair] += jnp.where(own, pltpu.roll(patch, turn, axis=1), 0.0)
            amplitude[pair] += jnp.where(own, pltpu.roll(shade, turn, axis=1), 0.0)
        return carry

    lax.fori_loop(0, peers, one_slot, 0, unroll=4)
    for load in loads:
        load.wait()

    arrays = (owner_of, cotangent, opd, amplitude, grad, turns_per, left1, left2, right1, right2)
    few = count <= FEW

    @pl.when(few)
    def _():
        wave_groups(GROUP_FEW, count, *arrays)

    @pl.when(jnp.logical_not(few))
    def _():
        wave_groups(GROUP, count, *arrays)

    def one_return(p, carry):
        sides = []
        for c in range(2):
            here = slot_place[2 * p + c]
            sides.append(pltpu.roll(grad[here >> 1], ((here & 1) ^ c) * SUB, axis=1))
        picked = jnp.where(lower, sides[0], sides[1])
        out[p] = jnp.where(shades[p] > 0.0, picked, 0.0).astype(jnp.bfloat16)
        return carry

    lax.fori_loop(0, peers, one_return, 0, unroll=4)


def round_up(value, step):
    return -(-value // step) * step


def wave_call(tables, message, cotangent, extent):
    peers = message.shape[0]
    lenses = cotangent.shape[0]
    pairs = max(round_up(lenses, 2 * GROUP), round_up(lenses, 2 * GROUP_FEW)) // 2
    vmem = pl.BlockSpec(memory_space=pltpu.VMEM)
    far = pl.BlockSpec(memory_space=pltpu.HBM)
    return pl.pallas_call(
        wave_kernel,
        out_shape=jax.ShapeDtypeStruct((peers, SUB, LANES), jnp.bfloat16),
        in_specs=[vmem, vmem] + [far] * len(tables),
        out_specs=vmem,
        scratch_shapes=[pltpu.VMEM(x.shape, x.dtype) for x in tables] + [
            pltpu.VMEM((2 * peers, LANES), jnp.int32),
            pltpu.SMEM((2 * peers, LANES), jnp.int32),
            pltpu.SMEM((lenses,), jnp.int32),
            pltpu.SMEM((2 * peers,), jnp.int32),
            pltpu.SMEM((2 * pairs + 1,), jnp.int32),
            pltpu.VMEM((pairs + 1, SUB, LANES), jnp.float32),
            pltpu.VMEM((pairs + 1, SUB, LANES), jnp.float32),
            pltpu.VMEM((pairs + 1, SUB, LANES), jnp.float32),
            pltpu.VMEM((peers, SUB, LANES), jnp.float32),
            pltpu.VMEM((extent, extent), jnp.float32),
            pltpu.SemaphoreType.DMA,
            pltpu.SemaphoreType.DMA((len(tables),)),
        ],
        compiler_params=pltpu.CompilerParams(vmem_limit_bytes=VMEM_LIMIT),
        name="wave_gradients",
    )(message, cotangent, *tables)


def place_kernel(entries, patches, out, heads, table, sem):
    peers = patches.shape[0]
    extent = out.shape[1]
    copy = read_table(entries, heads, table, sem)
    lane = lax.broadcasted_iota(jnp.int32, (WINDOW, LANES), 1)
    spare = jnp.zeros((WINDOW - SUB, LANES), jnp.float32)
    out[...] = jnp.zeros_like(out)
    copy.wait()

    def one_peer(p, carry):
        both = jnp.concatenate([patches[p].astype(jnp.float32), spare], axis=0)
        for c in range(2):
            seg, row, col = (table[2 * p + c, k] for k in (1, 3, 4))
            base, down = aligned(row, extent)
            moved = pltpu.roll(both, (col + LANES - SUB * c) & (LANES - 1), axis=1)
            moved = pltpu.roll(moved, down, axis=0)
            for half in range(2):
                j = lane + (half * LANES - col)
                kept = jnp.where((j >= 0) & (j < SUB), moved, 0.0)
                spot = (seg, pl.ds(base, WINDOW), pl.ds(half * LANES, LANES))
                out[spot] += kept
        return carry

    lax.fori_loop(0, peers, one_peer, 0, unroll=4)


def on_device(segment_maps, cotangent, wavelengths, intersections):
    peers = intersections.shape[0]
    segs, extent, _ = segment_maps.shape
    vmem = pl.BlockSpec(memory_space=pltpu.VMEM)
    table_space = [pltpu.VMEM((2 * peers, LANES), jnp.int32), pltpu.SMEM((2 * peers, LANES), jnp.int32)]
    params = pltpu.CompilerParams(vmem_limit_bytes=VMEM_LIMIT)

    message = pl.pallas_call(
        cut_kernel,
        out_shape=jax.ShapeDtypeStruct((peers, SUB + HEAD, LANES), jnp.bfloat16),
        in_specs=[vmem, pl.BlockSpec(memory_space=pltpu.HBM)],
        out_specs=vmem,
        scratch_shapes=[
            *table_space,
            pltpu.VMEM((segs, extent, extent), jnp.bfloat16),
            pltpu.VMEM((segs, extent, extent), jnp.float32),
            pltpu.SemaphoreType.DMA,
            pltpu.SemaphoreType.DMA((segs,)),
        ],
        compiler_params=params,
        name="cut_patches",
    )(intersections, segment_maps)
    tables = table_call(wavelengths)
    arriving = lax.all_to_all(message, "tile", split_axis=0, concat_axis=0, tiled=True)
    grads = wave_call(tables, arriving, cotangent, extent)
    returned = lax.all_to_all(grads, "tile", split_axis=0, concat_axis=0, tiled=True)
    return pl.pallas_call(
        place_kernel,
        out_shape=jax.ShapeDtypeStruct((segs, extent, extent), jnp.float32),
        in_specs=[vmem, vmem],
        out_specs=vmem,
        scratch_shapes=[*table_space, pltpu.SemaphoreType.DMA],
        compiler_params=params,
        name="place_gradients",
    )(intersections, returned)


def solution(mesh):
    return jax.shard_map(
        on_device,
        mesh=mesh,
        in_specs=(
            P(("case", "tile"), None, None),
            P(("case", "tile"), None, None),
            P(),
            P(("case", "tile"), None, None),
        ),
        out_specs=P(("case", "tile"), None, None),
        check_vma=False,
    )
```

```python
import functools
import math

import jax
import jax.numpy as jnp
from jax import lax
from jax.experimental import pallas as pl
from jax.experimental.pallas import tpu as pltpu
from jax.sharding import PartitionSpec as P

SUB = 64
LANES = 2 * SUB
HEAD = 8
HEAD_ROWS = 16
WINDOW = SUB + 8
RIGHT1, RIGHT2, LEFT, WAVE_ROWS = 0, 2 * LANES, 4 * LANES, 5 * LANES
FIELDS = 5
SAMPLING = 0.5
GROUP = 4
GROUP_FEW = 5
FEW = 20
VMEM = 64 * 1024 * 1024
VMEM_LIMIT = 48 * 1024 * 1024
FAR_ROWS = 40960

LEAD = -0.7843722149521581
SINE = tuple(a / LEAD for a in (4.442867901299065, -7.307443351304121, 3.594787401596918))
COSINE = tuple(a / LEAD for a in (1.4142040792740376, -6.9776419299271595, 5.715236658714806, -1.7283430271755356))


FINE_SINE = (4.442882834139933, -7.308241153900929, 3.6062889473067714, -0.8457635292158341, 0.10920561913977103)
FINE_COSINE = (1.4142134965588182, -6.978850987079529, 5.739461141869117, -1.8835627683436942, 0.3106976855933321)


def horner(coefficients, z):
    total = coefficients[-1]
    for coefficient in coefficients[-2::-1]:
        total = total * z + coefficient
    return total


def half_turn(turns):
    r = turns - jnp.round(turns)
    z = r * r
    sine = (((z + SINE[2]) * z + SINE[1]) * z + SINE[0]) * r
    cosine = ((COSINE[3] * z + COSINE[2]) * z + COSINE[1]) * z + COSINE[0]
    return sine, cosine


def row_limit(rows, first, extent):
    i = lax.broadcasted_iota(jnp.int32, (rows, LANES), 0) + first
    down = jnp.abs(2 * i - (extent - 1))
    return jnp.where(8 * down <= 7 * (extent - 1), 7 * (extent - 1) - 4 * down, -1)


def aligned(row, extent):
    base = pl.multiple_of(jnp.minimum(row // 8 * 8, extent - WINDOW), 8)
    return base, row - base


def sideways(first, extent):
    j = lax.broadcasted_iota(jnp.int32, (1, LANES), 1) + first
    return 7 * jnp.abs(2 * j - (extent - 1))


def window(image, row, col, extent, side):
    base, down = aligned(row, extent)
    left = image[pl.ds(base, WINDOW), pl.ds(0, LANES)]
    right = image[pl.ds(base, WINDOW), pl.ds(LANES, LANES)]
    lane = lax.broadcasted_iota(jnp.int32, (WINDOW, LANES), 1)
    both = jnp.where(lane >= col, left, right)
    both = pltpu.roll(both, jnp.where(down == 0, 0, WINDOW - down), axis=0)[:SUB]
    return pltpu.roll(both, (2 * LANES + SUB * side - col) & (LANES - 1), axis=1)


def fill_mask(mask):
    extent = mask.shape[0]
    chunk = 32
    for row in range(0, extent, chunk):
        limit = row_limit(chunk, row, extent)
        for half in range(extent // LANES):
            inside = sideways(half * LANES, extent) <= limit
            mask[pl.ds(row, chunk), pl.ds(half * LANES, LANES)] = jnp.where(inside, 1.0, 0.0)


def read_table(entries, heads, table, sem):
    for k in range(FIELDS):
        heads[pl.ds(2 * k, 2), pl.ds(0, entries.shape[2])] = entries[k]
    copy = pltpu.make_async_copy(heads, table, sem)
    copy.start()
    return copy


def cut_kernel(entries_far, maps, out, entries, heads, table, raw, masked, sem, map_sems):
    peers = out.shape[0]
    segs, extent, _ = maps.shape
    first = pltpu.make_async_copy(entries_far, entries, sem)
    first.start()
    loads = [pltpu.make_async_copy(maps.at[s], raw.at[s], map_sems.at[s]) for s in range(segs)]
    for load in loads:
        load.start()
    lower = lax.broadcasted_iota(jnp.int32, (SUB, LANES), 1) < SUB
    first.wait()
    copy = read_table(entries, heads, table, sem)
    rows = jnp.transpose(heads[...].astype(jnp.float32)).astype(jnp.bfloat16)
    for p in range(peers):
        out[p, pl.ds(SUB, 1), pl.ds(0, HEAD_ROWS)] = rows[p : p + 1]
    chunk = 32
    for s in range(segs):
        loads[s].wait()
        for row in range(0, extent, chunk):
            limit = row_limit(chunk, row, extent)
            for half in range(extent // LANES):
                inside = sideways(half * LANES, extent) <= limit
                spot = (s, pl.ds(row, chunk), pl.ds(half * LANES, LANES))
                masked[spot] = jnp.where(inside, raw[spot].astype(jnp.float32), 0.0)
    copy.wait()

    def one_peer(p, carry):
        sides = []
        for c in range(2):
            live, seg, row, col = (table[2 * k + c, p] for k in (0, 1, 3, 4))
            piece = window(masked.at[seg], row, col, extent, c)
            sides.append(piece * live.astype(jnp.float32))
        out[p, pl.ds(0, SUB), :] = jnp.where(lower, sides[0], sides[1]).astype(jnp.bfloat16)
        return carry

    lax.fori_loop(0, peers, one_peer, 0, unroll=8)


def slab_rows(waves, lenses):
    return waves * WAVE_ROWS + round_up(lenses, 2) // 2 * SUB


def weight_spot(lens, waves):
    return pl.ds(waves * WAVE_ROWS + (lens >> 1) * SUB, SUB), pl.ds(pl.multiple_of((lens & 1) * LANES, LANES), LANES)


def table_kernel(waves_ref, cotangent, slab_far, slab, sem):
    waves = waves_ref.shape[0]
    position = lax.broadcasted_iota(jnp.int32, (SUB, LANES), 0) - SUB // 2
    lane = lax.broadcasted_iota(jnp.int32, (SUB, LANES), 1)
    across = (lane & (SUB - 1)) - SUB // 2
    product = (position * across).astype(jnp.float32) * (-SAMPLING / SUB)
    lower = lane < SUB

    def one_table(w, carry):
        turns = product * (1.0 / jnp.full((1, LANES), waves_ref[w], jnp.float32))
        r = turns - jnp.round(turns)
        z = r * r
        sine = horner(FINE_SINE, z) * r
        real = 1.0 - sine * sine
        imag = sine * horner(FINE_COSINE, z)

        def put(row, side, value):
            slab[pl.ds(w * WAVE_ROWS + row, SUB), pl.ds(side * LANES, LANES)] = value.astype(jnp.bfloat16)

        put(LEFT, 0, jnp.where(lower, real, -imag))
        put(LEFT + SUB, 0, jnp.where(lower, imag, real))
        put(LEFT, 1, jnp.where(lower, real, imag))
        put(LEFT + SUB, 1, jnp.where(lower, -imag, real))
        for h in range(2):
            own = lower if h == 0 else ~lower
            re = jnp.where(own, real, 0.0)
            im = jnp.where(own, imag, 0.0)
            first, second = h * SUB, LANES + h * SUB
            put(RIGHT1 + first, 0, re)
            put(RIGHT1 + first, 1, im)
            put(RIGHT1 + second, 0, -im)
            put(RIGHT1 + second, 1, re)
            put(RIGHT2 + first, 0, re)
            put(RIGHT2 + first, 1, -im)
            put(RIGHT2 + second, 0, im)
            put(RIGHT2 + second, 1, re)
        return carry

    lax.fori_loop(0, waves, one_table, 0)
    for l in range(cotangent.shape[0]):
        own = cotangent[l].astype(jnp.float32) * (2.0 / (waves * SUB))
        slab[weight_spot(l, waves)] = jnp.concatenate([own, own], axis=1).astype(jnp.bfloat16)
    copy = pltpu.make_async_copy(slab, slab_far.at[pl.ds(0, slab.shape[0]), :], sem)
    copy.start()
    copy.wait()


def table_call(wavelengths, cotangent):
    vmem = pl.BlockSpec(memory_space=pltpu.VMEM)
    rows = slab_rows(wavelengths.shape[0], cotangent.shape[0])
    return pl.pallas_call(
        table_kernel,
        out_shape=jax.ShapeDtypeStruct((max(rows, FAR_ROWS), 2 * LANES), jnp.bfloat16),
        in_specs=[pl.BlockSpec(memory_space=pltpu.SMEM), vmem],
        out_specs=pl.BlockSpec(memory_space=pltpu.HBM),
        scratch_shapes=[pltpu.VMEM((rows, 2 * LANES), jnp.bfloat16), pltpu.SemaphoreType.DMA],
        compiler_params=pltpu.CompilerParams(vmem_limit_bytes=VMEM_LIMIT),
        cost_estimate=pl.CostEstimate(flops=10_000_000, bytes_accessed=6_000_000, transcendentals=0),
        name="lens_tables",
    )(wavelengths, cotangent)


def wave_groups(group, count, owner_of, opd, amplitude, grad, turns_per, slab):
    waves = turns_per.shape[0]
    lower = lax.broadcasted_iota(jnp.int32, (SUB, LANES), 1) < SUB

    def stack(res, ims):
        top = jnp.concatenate([x.astype(jnp.bfloat16) for x in res], axis=1)
        low = jnp.concatenate([x.astype(jnp.bfloat16) for x in ims], axis=1)
        return jnp.concatenate([top, low], axis=0)

    def line(x):
        x = x.astype(jnp.bfloat16)
        rows = []
        for i in range(group):
            at = slice(LANES * i, LANES * (i + 1))
            rows.append(jnp.concatenate([x[:SUB, at], x[SUB:, at]], axis=1))
        return jnp.concatenate(rows, axis=0)

    def one_group(g, carry):
        weights, scaled = [], []
        totals = [None] * group
        for i in range(group):
            k = (g * group + i) * 2
            scaled.append(amplitude[g * group + i] * LEAD**2)
            pieces = [slab[weight_spot(owner_of[k + h], waves)].astype(jnp.float32) for h in range(2)]
            weights.append(jnp.where(lower, *pieces))

        def field(w, state):
            scale = turns_per[w][0:1]
            reals, imags = [], []
            for i in range(group):
                sine, cosine = half_turn(opd[g * group + i] * scale)
                part = scaled[i] * sine
                reals.append(amplitude[g * group + i] - part * sine)
                imags.append(part * cosine)
            return reals, imags, stack(reals, imags)

        def pupil_rows(w, state):
            reals, imags, e = state
            return reals, imags, line(jnp.dot(slab[pl.ds(w * WAVE_ROWS + LEFT, LANES), pl.ds(0, LANES)], e, preferred_element_type=jnp.float32))

        def pupil_columns(w, state):
            reals, imags, p = state
            f = jnp.dot(p, slab[pl.ds(w * WAVE_ROWS + RIGHT1, 2 * LANES), :], preferred_element_type=jnp.float32)
            held = [[], []]
            for i in range(group):
                for h in range(2):
                    held[h].append(f[SUB * i : SUB * (i + 1), LANES * h : LANES * (h + 1)] * weights[i])
            return reals, imags, stack(*held)

        def focal_rows(w, state):
            reals, imags, held = state
            return reals, imags, line(jnp.dot(slab[pl.ds(w * WAVE_ROWS + LEFT, LANES), pl.ds(LANES, LANES)], held, preferred_element_type=jnp.float32))

        def focal_columns(w, state):
            reals, imags, q = state
            b = jnp.dot(q, slab[pl.ds(w * WAVE_ROWS + RIGHT2, 2 * LANES), :], preferred_element_type=jnp.float32)
            factor = turns_per[w][0:1] * (2.0 * math.pi / SUB)
            for i in range(group):
                back = b[SUB * i : SUB * (i + 1)]
                term = factor * (reals[i] * back[:, LANES:] - imags[i] * back[:, :LANES])
                totals[i] = term if totals[i] is None else totals[i] + term

        stages = (field, pupil_rows, pupil_columns, focal_rows, focal_columns)
        states = [None] * waves
        for t in range(waves + len(stages) - 1):
            for k, stage in enumerate(stages):
                if 0 <= t - k < waves:
                    states[t - k] = stage(t - k, states[t - k])
        for i in range(group):
            grad[g * group + i] = totals[i]
        return carry

    lax.fori_loop(0, (count + 2 * group - 1) // (2 * group), one_group, 0)


def wave_kernel(
    lenses, waves_ref, message, slab_far, out,
    slab, turns_per, heads, table, place, slot_place, owner_of, opd, amplitude, grad, shades, mask, sem, slab_sem,
):
    peers = message.shape[0]
    pairs = opd.shape[0] - 1
    extent = mask.shape[0]
    dead_place = 2 * pairs

    load = pltpu.make_async_copy(slab_far.at[pl.ds(0, slab.shape[0]), :], slab, slab_sem)
    load.start()
    for w in range(waves_ref.shape[0]):
        turns_per[w] = 1.0 / jnp.full((8, LANES), waves_ref[w], jnp.float32)
    for p in range(peers):
        head = message[p, pl.ds(SUB, HEAD), :].astype(jnp.float32)[0:1]
        heads[pl.ds(p, 1), :] = head.astype(jnp.int32)
    copy = pltpu.make_async_copy(heads, table, sem)
    copy.start()
    fill_mask(mask)
    opd[...] = jnp.zeros_like(opd)
    amplitude[...] = jnp.zeros_like(amplitude)
    lane = lax.broadcasted_iota(jnp.int32, (SUB, LANES), 1)
    lower = lane < SUB
    for l in range(lenses):
        place[l] = -1
    for k in range(dead_place + 1):
        owner_of[k] = 0
    copy.wait()

    def one_place(i, count):
        p, c = i >> 1, i & 1
        live = table[p, c] == 1
        lens = table[p, 4 + c]
        before = place[lens]
        fresh = live & (before < 0)
        here = jnp.where(fresh, count, before)
        place[lens] = here
        owner_of[count] = jnp.where(fresh, lens, 0)
        slot_place[i] = jnp.where(live, here, dead_place)
        return count + fresh.astype(jnp.int32)

    count = lax.fori_loop(0, 2 * peers, one_place, 0, unroll=4)

    def one_slot(p, carry):
        patch = message[p, pl.ds(0, SUB), :].astype(jnp.float32)
        sides = []
        for c in range(2):
            live, row, col = (table[p, 2 * k + c] for k in (0, 3, 4))
            sides.append(window(mask, row, col, extent, c) * live.astype(jnp.float32))
        shade = jnp.where(lower, sides[0], sides[1])
        shades[p] = shade
        for c in range(2):
            here = slot_place[2 * p + c]
            pair = here >> 1
            half = here & 1
            turn = (half ^ c) * SUB
            own = (lane >> 6) == half
            opd[pair] += jnp.where(own, pltpu.roll(patch, turn, axis=1), 0.0)
            amplitude[pair] += jnp.where(own, pltpu.roll(shade, turn, axis=1), 0.0)
        return carry

    lax.fori_loop(0, peers, one_slot, 0, unroll=4)
    load.wait()

    arrays = (owner_of, opd, amplitude, grad, turns_per, slab)
    few = count <= FEW

    @pl.when(few)
    def _():
        wave_groups(GROUP_FEW, count, *arrays)

    @pl.when(jnp.logical_not(few))
    def _():
        wave_groups(GROUP, count, *arrays)

    def one_return(p, carry):
        sides = []
        for c in range(2):
            here = slot_place[2 * p + c]
            sides.append(pltpu.roll(grad[here >> 1], ((here & 1) ^ c) * SUB, axis=1))
        picked = jnp.where(lower, sides[0], sides[1])
        out[p] = jnp.where(shades[p] > 0.0, picked, 0.0).astype(jnp.bfloat16)
        return carry

    lax.fori_loop(0, peers, one_return, 0, unroll=4)


def all_but(size):
    return pltpu.CompilerParams(vmem_limit_bytes=max(VMEM - size - 64 * 1024, VMEM_LIMIT))


def round_up(value, step):
    return -(-value // step) * step


def wave_call(wavelengths, tables, message, lenses, extent):
    peers = message.shape[0]
    pairs = max(round_up(lenses, 2 * GROUP), round_up(lenses, 2 * GROUP_FEW)) // 2
    vmem = pl.BlockSpec(memory_space=pltpu.VMEM)
    far = pl.BlockSpec(memory_space=pltpu.HBM)
    return pl.pallas_call(
        functools.partial(wave_kernel, lenses),
        out_shape=jax.ShapeDtypeStruct((peers, SUB, LANES), jnp.bfloat16),
        in_specs=[pl.BlockSpec(memory_space=pltpu.SMEM), vmem, far],
        out_specs=vmem,
        scratch_shapes=[
            pltpu.VMEM((slab_rows(wavelengths.shape[0], lenses), 2 * LANES), jnp.bfloat16),
            pltpu.VMEM((wavelengths.shape[0], 8, LANES), jnp.float32),
            pltpu.VMEM((peers, LANES), jnp.int32),
            pltpu.SMEM((peers, LANES), jnp.int32),
            pltpu.SMEM((lenses,), jnp.int32),
            pltpu.SMEM((2 * peers,), jnp.int32),
            pltpu.SMEM((2 * pairs + 1,), jnp.int32),
            pltpu.VMEM((pairs + 1, SUB, LANES), jnp.float32),
            pltpu.VMEM((pairs + 1, SUB, LANES), jnp.float32),
            pltpu.VMEM((pairs + 1, SUB, LANES), jnp.float32),
            pltpu.VMEM((peers, SUB, LANES), jnp.float32),
            pltpu.VMEM((extent, extent), jnp.float32),
            pltpu.SemaphoreType.DMA,
            pltpu.SemaphoreType.DMA,
        ],
        compiler_params=pltpu.CompilerParams(vmem_limit_bytes=VMEM_LIMIT),
        name="wave_gradients",
    )(wavelengths, message, tables)


def place_kernel(entries, patches, out, heads, table, sem):
    peers = patches.shape[0]
    extent = out.shape[1]
    copy = read_table(entries, heads, table, sem)
    lane = lax.broadcasted_iota(jnp.int32, (WINDOW, LANES), 1)
    spare = jnp.zeros((WINDOW - SUB, LANES), jnp.float32)
    out[...] = jnp.zeros_like(out)
    copy.wait()

    def one_peer(p, carry):
        both = jnp.concatenate([patches[p].astype(jnp.float32), spare], axis=0)
        for c in range(2):
            seg, row, col = (table[2 * k + c, p] for k in (1, 3, 4))
            base, down = aligned(row, extent)
            moved = pltpu.roll(both, (col + LANES - SUB * c) & (LANES - 1), axis=1)
            moved = pltpu.roll(moved, down, axis=0)
            for half in range(2):
                j = lane + (half * LANES - col)
                kept = jnp.where((j >= 0) & (j < SUB), moved, 0.0)
                spot = (seg, pl.ds(base, WINDOW), pl.ds(half * LANES, LANES))
                out[spot] += kept
        return carry

    lax.fori_loop(0, peers, one_peer, 0, unroll=4)


def on_device(segment_maps, cotangent, wavelengths, intersections):
    peers = intersections.shape[0]
    segs, extent, _ = segment_maps.shape
    vmem = pl.BlockSpec(memory_space=pltpu.VMEM)
    entries = jnp.transpose(intersections, (2, 1, 0))
    table_shape = (HEAD_ROWS, round_up(peers, LANES))
    table_space = [pltpu.VMEM(table_shape, jnp.int32), pltpu.SMEM(table_shape, jnp.int32)]
    params = pltpu.CompilerParams(vmem_limit_bytes=VMEM_LIMIT)

    message = pl.pallas_call(
        cut_kernel,
        out_shape=jax.ShapeDtypeStruct((peers, SUB + HEAD, LANES), jnp.bfloat16),
        in_specs=[pl.BlockSpec(memory_space=pl.ANY)] * 2,
        out_specs=vmem,
        scratch_shapes=[
            pltpu.VMEM(entries.shape, jnp.int32),
            *table_space,
            pltpu.VMEM((segs, extent, extent), jnp.bfloat16),
            pltpu.VMEM((segs, extent, extent), jnp.float32),
            pltpu.SemaphoreType.DMA,
            pltpu.SemaphoreType.DMA((segs,)),
        ],
        compiler_params=all_but(peers * (SUB + HEAD) * LANES * 2),
        name="cut_patches",
    )(entries, segment_maps)
    tables = table_call(wavelengths, cotangent)
    arriving = lax.all_to_all(message, "tile", split_axis=0, concat_axis=0, tiled=True)
    grads = wave_call(wavelengths, tables, arriving, cotangent.shape[0], extent)
    returned = lax.all_to_all(grads, "tile", split_axis=0, concat_axis=0, tiled=True)
    return pl.pallas_call(
        place_kernel,
        out_shape=jax.ShapeDtypeStruct((segs, extent, extent), jnp.float32),
        in_specs=[vmem, vmem],
        out_specs=vmem,
        scratch_shapes=[*table_space, pltpu.SemaphoreType.DMA],
        compiler_params=params,
        name="place_gradients",
    )(entries, returned)


def solution(mesh):
    return jax.shard_map(
        on_device,
        mesh=mesh,
        in_specs=(
            P(("case", "tile"), None, None),
            P(("case", "tile"), None, None),
            P(),
            P(("case", "tile"), None, None),
        ),
        out_specs=P(("case", "tile"), None, None),
        check_vma=False,
    )
```

```python
import functools
import math

import jax
import jax.numpy as jnp
from jax import lax
from jax.experimental import pallas as pl
from jax.experimental.pallas import tpu as pltpu
from jax.sharding import PartitionSpec as P

SUB = 64
LANES = 2 * SUB
HEAD = 8
HEAD_ROWS = 16
WINDOW = SUB + 8
RIGHT1, RIGHT2, LEFT, WAVE_ROWS = 0, 2 * LANES, 4 * LANES, 5 * LANES
FIELDS = 5
SAMPLING = 0.5
SIZES = ((5,), (4, 3), (5, 4), (5, 5))
SIZES_MANY = (4,)
BATCH = 8
VMEM = 64 * 1024 * 1024
VMEM_LIMIT = 48 * 1024 * 1024
FAR_ROWS = 40960

LEAD = -0.7843722149521581
SINE = tuple(a / LEAD for a in (4.442867901299065, -7.307443351304121, 3.594787401596918))
COSINE = tuple(a / LEAD for a in (1.4142040792740376, -6.9776419299271595, 5.715236658714806, -1.7283430271755356))


FINE_SINE = (4.442882834139933, -7.308241153900929, 3.6062889473067714, -0.8457635292158341, 0.10920561913977103)
FINE_COSINE = (1.4142134965588182, -6.978850987079529, 5.739461141869117, -1.8835627683436942, 0.3106976855933321)


def horner(coefficients, z):
    total = coefficients[-1]
    for coefficient in coefficients[-2::-1]:
        total = total * z + coefficient
    return total


def half_turn(turns):
    r = turns - jnp.round(turns)
    z = r * r
    sine = (((z + SINE[2]) * z + SINE[1]) * z + SINE[0]) * r
    cosine = ((COSINE[3] * z + COSINE[2]) * z + COSINE[1]) * z + COSINE[0]
    return sine, cosine


def row_limit(rows, first, extent):
    i = lax.broadcasted_iota(jnp.int32, (rows, LANES), 0) + first
    down = jnp.abs(2 * i - (extent - 1))
    return jnp.where(8 * down <= 7 * (extent - 1), 7 * (extent - 1) - 4 * down, -1)


def aligned(row, extent):
    base = pl.multiple_of(jnp.minimum(row // 8 * 8, extent - WINDOW), 8)
    return base, row - base


def sideways(first, extent):
    j = lax.broadcasted_iota(jnp.int32, (1, LANES), 1) + first
    return 7 * jnp.abs(2 * j - (extent - 1))


def window(image, row, col, extent, side):
    base, down = aligned(row, extent)
    left = image[pl.ds(base, WINDOW), pl.ds(0, LANES)]
    right = image[pl.ds(base, WINDOW), pl.ds(LANES, LANES)]
    lane = lax.broadcasted_iota(jnp.int32, (WINDOW, LANES), 1)
    both = jnp.where(lane >= col, left, right)
    both = pltpu.roll(both, jnp.where(down == 0, 0, WINDOW - down), axis=0)[:SUB]
    return pltpu.roll(both, (2 * LANES + SUB * side - col) & (LANES - 1), axis=1)


def fill_mask(mask):
    extent = mask.shape[0]
    chunk = 32
    for row in range(0, extent, chunk):
        limit = row_limit(chunk, row, extent)
        for half in range(extent // LANES):
            inside = sideways(half * LANES, extent) <= limit
            mask[pl.ds(row, chunk), pl.ds(half * LANES, LANES)] = jnp.where(inside, 1.0, 0.0)


def read_table(entries, heads, table, sem):
    for k in range(FIELDS):
        heads[pl.ds(2 * k, 2), pl.ds(0, entries.shape[2])] = entries[k]
    copy = pltpu.make_async_copy(heads, table, sem)
    copy.start()
    return copy


def cut_kernel(entries_far, maps, out_far, entries, heads, table, raw, masked, out, sem, map_sems, out_sems):
    peers = out.shape[0]
    segs, extent, _ = maps.shape
    first = pltpu.make_async_copy(entries_far, entries, sem)
    first.start()
    loads = [pltpu.make_async_copy(maps.at[s], raw.at[s], map_sems.at[s]) for s in range(segs)]
    for load in loads:
        load.start()
    lower = lax.broadcasted_iota(jnp.int32, (SUB, LANES), 1) < SUB
    first.wait()
    copy = read_table(entries, heads, table, sem)
    rows = jnp.transpose(heads[...].astype(jnp.float32)).astype(jnp.bfloat16)
    for p in range(peers):
        out[p, pl.ds(SUB, 1), pl.ds(0, HEAD_ROWS)] = rows[p : p + 1]
    for load in loads:
        load.wait()
    chunk = 32
    for row in range(0, extent, chunk):
        limit = row_limit(chunk, row, extent)
        for half in range(extent // LANES):
            inside = sideways(half * LANES, extent) <= limit
            for s in range(segs):
                spot = (s, pl.ds(row, chunk), pl.ds(half * LANES, LANES))
                masked[spot] = jnp.where(inside, raw[spot].astype(jnp.float32), 0.0)
    copy.wait()

    def one_peer(p, carry):
        sides = []
        for c in range(2):
            live, seg, row, col = (table[2 * k + c, p] for k in (0, 1, 3, 4))
            piece = window(masked.at[seg], row, col, extent, c)
            sides.append(piece * live.astype(jnp.float32))
        out[p, pl.ds(0, SUB), :] = jnp.where(lower, sides[0], sides[1]).astype(jnp.bfloat16)
        return carry

    batches = out_sems.shape[0]
    batch = peers // batches

    def send(b):
        part = pl.ds(b * batch, batch)
        return pltpu.make_async_copy(out.at[part], out_far.at[part], out_sems.at[b])

    for b in range(batches):
        lax.fori_loop(b * batch, (b + 1) * batch, one_peer, 0, unroll=True)
        send(b).start()
    for b in range(batches):
        send(b).wait()


def slab_rows(waves, lenses):
    return waves * WAVE_ROWS + round_up(lenses, 2) // 2 * SUB


def weight_spot(lens, waves):
    return pl.ds(waves * WAVE_ROWS + (lens >> 1) * SUB, SUB), pl.ds(pl.multiple_of((lens & 1) * LANES, LANES), LANES)


def table_kernel(waves_ref, cotangent, slab_far, slab, sem):
    waves = waves_ref.shape[0]
    position = lax.broadcasted_iota(jnp.int32, (SUB, LANES), 0) - SUB // 2
    lane = lax.broadcasted_iota(jnp.int32, (SUB, LANES), 1)
    across = (lane & (SUB - 1)) - SUB // 2
    product = (position * across).astype(jnp.float32) * (-SAMPLING / SUB)
    lower = lane < SUB

    def one_table(w, carry):
        turns = product * (1.0 / jnp.full((1, LANES), waves_ref[w], jnp.float32))
        r = turns - jnp.round(turns)
        z = r * r
        sine = horner(FINE_SINE, z) * r
        real = 1.0 - sine * sine
        imag = sine * horner(FINE_COSINE, z)

        def put(row, side, value):
            slab[pl.ds(w * WAVE_ROWS + row, SUB), pl.ds(side * LANES, LANES)] = value.astype(jnp.bfloat16)

        put(LEFT, 0, jnp.where(lower, real, -imag))
        put(LEFT + SUB, 0, jnp.where(lower, imag, real))
        put(LEFT, 1, jnp.where(lower, real, imag))
        put(LEFT + SUB, 1, jnp.where(lower, -imag, real))
        for h in range(2):
            own = lower if h == 0 else ~lower
            re = jnp.where(own, real, 0.0)
            im = jnp.where(own, imag, 0.0)
            first, second = h * SUB, LANES + h * SUB
            put(RIGHT1 + first, 0, re)
            put(RIGHT1 + first, 1, im)
            put(RIGHT1 + second, 0, -im)
            put(RIGHT1 + second, 1, re)
            put(RIGHT2 + first, 0, re)
            put(RIGHT2 + first, 1, -im)
            put(RIGHT2 + second, 0, im)
            put(RIGHT2 + second, 1, re)
        return carry

    lax.fori_loop(0, waves, one_table, 0)
    for l in range(cotangent.shape[0]):
        own = cotangent[l].astype(jnp.float32) * (2.0 / (waves * SUB))
        slab[weight_spot(l, waves)] = jnp.concatenate([own, own], axis=1).astype(jnp.bfloat16)
    copy = pltpu.make_async_copy(slab, slab_far.at[pl.ds(0, slab.shape[0]), :], sem)
    copy.start()
    copy.wait()


def table_call(wavelengths, cotangent):
    vmem = pl.BlockSpec(memory_space=pltpu.VMEM)
    rows = slab_rows(wavelengths.shape[0], cotangent.shape[0])
    return pl.pallas_call(
        table_kernel,
        out_shape=jax.ShapeDtypeStruct((max(rows, FAR_ROWS), 2 * LANES), jnp.bfloat16),
        in_specs=[pl.BlockSpec(memory_space=pltpu.SMEM), vmem],
        out_specs=pl.BlockSpec(memory_space=pltpu.HBM),
        scratch_shapes=[pltpu.VMEM((rows, 2 * LANES), jnp.bfloat16), pltpu.SemaphoreType.DMA],
        compiler_params=pltpu.CompilerParams(vmem_limit_bytes=VMEM_LIMIT),
        cost_estimate=pl.CostEstimate(flops=10_000_000, bytes_accessed=6_000_000, transcendentals=0),
        name="lens_tables",
    )(wavelengths, cotangent)


def wave_groups(sizes, count, owner_of, opd, amplitude, grad, turns_per, slab):
    waves = turns_per.shape[0]
    lower = lax.broadcasted_iota(jnp.int32, (SUB, LANES), 1) < SUB

    def stack(res, ims):
        top = jnp.concatenate([x.astype(jnp.bfloat16) for x in res], axis=1)
        low = jnp.concatenate([x.astype(jnp.bfloat16) for x in ims], axis=1)
        return jnp.concatenate([top, low], axis=0)

    def line(x):
        x = x.astype(jnp.bfloat16)
        rows = []
        for i in range(x.shape[1] // LANES):
            at = slice(LANES * i, LANES * (i + 1))
            rows.append(jnp.concatenate([x[:SUB, at], x[SUB:, at]], axis=1))
        return jnp.concatenate(rows, axis=0)

    def begin(start, size):
        weights, scaled = [], []
        for i in range(size):
            k = (start + i) * 2
            scaled.append(amplitude[start + i] * LEAD**2)
            pieces = [slab[weight_spot(owner_of[k + h], waves)].astype(jnp.float32) for h in range(2)]
            weights.append(jnp.where(lower, *pieces))
        return start, weights, scaled, [None] * size

    def field(w, own, state):
        start, _, scaled, _ = own
        scale = turns_per[w][0:1]
        reals, imags = [], []
        for i in range(len(scaled)):
            sine, cosine = half_turn(opd[start + i] * scale)
            part = scaled[i] * sine
            reals.append(amplitude[start + i] - part * sine)
            imags.append(part * cosine)
        return reals, imags, stack(reals, imags)

    def pupil_rows(w, own, state):
        reals, imags, e = state
        table = slab[pl.ds(w * WAVE_ROWS + LEFT, LANES), pl.ds(0, LANES)]
        return reals, imags, line(jnp.dot(table, e, preferred_element_type=jnp.float32))

    def pupil_columns(w, own, state):
        reals, imags, p = state
        weights = own[1]
        table = slab[pl.ds(w * WAVE_ROWS + RIGHT1, 2 * LANES), :]
        f = jnp.dot(p, table, preferred_element_type=jnp.float32)
        held = [[], []]
        for i in range(len(weights)):
            for h in range(2):
                held[h].append(f[SUB * i : SUB * (i + 1), LANES * h : LANES * (h + 1)] * weights[i])
        return reals, imags, stack(*held)

    def focal_rows(w, own, state):
        reals, imags, held = state
        table = slab[pl.ds(w * WAVE_ROWS + LEFT, LANES), pl.ds(LANES, LANES)]
        return reals, imags, line(jnp.dot(table, held, preferred_element_type=jnp.float32))

    def focal_columns(w, own, state):
        reals, imags, q = state
        start, _, _, totals = own
        table = slab[pl.ds(w * WAVE_ROWS + RIGHT2, 2 * LANES), :]
        b = jnp.dot(q, table, preferred_element_type=jnp.float32)
        factor = turns_per[w][0:1] * (2.0 * math.pi / SUB)
        for i in range(len(totals)):
            back = b[SUB * i : SUB * (i + 1)]
            term = factor * (reals[i] * back[:, LANES:] - imags[i] * back[:, :LANES])
            totals[i] = term if totals[i] is None else totals[i] + term
            if w == waves - 1:
                grad[start + i] = totals[i]

    stages = (field, pupil_rows, pupil_columns, focal_rows, focal_columns)

    def some_groups(turn, carry):
        owns, states = {}, {}
        items = len(sizes) * waves
        for t in range(items + len(stages) - 1):
            for k, stage in enumerate(stages):
                n = t - k
                if 0 <= n < items:
                    g, w = divmod(n, waves)
                    if g not in owns:
                        owns[g] = begin(turn * sum(sizes) + sum(sizes[:g]), sizes[g])
                    states[n] = stage(w, owns[g], states.pop(n, None))
        return carry

    step = 2 * sum(sizes)
    lax.fori_loop(0, (count + step - 1) // step, some_groups, 0)


def wave_kernel(
    lenses, waves_far, message, slab_far, out,
    waves_ref, slab, turns_per, heads, table, place, slot_place, owner_of, opd, amplitude, grad, shades, mask, sem, slab_sem, waves_sem,
):
    peers = message.shape[0]
    pairs = opd.shape[0] - 1
    extent = mask.shape[0]
    dead_place = 2 * pairs

    load = pltpu.make_async_copy(slab_far.at[pl.ds(0, slab.shape[0]), :], slab, slab_sem)
    load.start()
    waves_load = pltpu.make_async_copy(waves_far, waves_ref, waves_sem)
    waves_load.start()
    for p in range(peers):
        head = message[p, pl.ds(SUB, HEAD), :].astype(jnp.float32)[0:1]
        heads[pl.ds(p, 1), :] = head.astype(jnp.int32)
    copy = pltpu.make_async_copy(heads, table, sem)
    copy.start()
    fill_mask(mask)
    opd[...] = jnp.zeros_like(opd)
    amplitude[...] = jnp.zeros_like(amplitude)
    lane = lax.broadcasted_iota(jnp.int32, (SUB, LANES), 1)
    lower = lane < SUB
    row_lane = lax.broadcasted_iota(jnp.int32, (1, LANES), 1) >> 6
    for l in range(lenses):
        place[l] = -1
    for k in range(dead_place + 1):
        owner_of[k] = 0
    copy.wait()

    def one_slot(p, count):
        patch = message[p, pl.ds(0, SUB), :].astype(jnp.float32)
        sides, heres = [], []
        for c in range(2):
            live, lens, row, col = (table[p, 2 * k + c] for k in (0, 2, 3, 4))
            sides.append(window(mask, row, col, extent, c) * live.astype(jnp.float32))
            before = place[lens]
            fresh = (live == 1) & (before < 0)
            here = jnp.where(fresh, count, before)
            place[lens] = here
            owner_of[count] = jnp.where(fresh, lens, 0)
            count = count + fresh.astype(jnp.int32)
            heres.append(jnp.where(live == 1, here, dead_place))
            slot_place[2 * p + c] = heres[c]
        shade = jnp.where(lower, sides[0], sides[1])
        shades[p] = shade
        for c in range(2):
            pair = heres[c] >> 1
            half = heres[c] & 1
            turn = (half ^ c) * SUB
            own = (row_lane == half).astype(jnp.float32)
            opd[pair] += pltpu.roll(patch, turn, axis=1) * own
            amplitude[pair] += pltpu.roll(shade, turn, axis=1) * own
        return count

    count = lax.fori_loop(0, peers, one_slot, 0, unroll=8)
    waves_load.wait()
    for w in range(waves_ref.shape[0]):
        turns_per[w] = 1.0 / jnp.full((8, LANES), waves_ref[w], jnp.float32)
    load.wait()

    arrays = (owner_of, opd, amplitude, grad, turns_per, slab)
    floor = 0
    for sizes in SIZES:
        ceiling = 2 * sum(sizes)

        @pl.when((count > floor) & (count <= ceiling))
        def _(sizes=sizes):
            wave_groups(sizes, count, *arrays)

        floor = ceiling

    @pl.when(count > floor)
    def _():
        wave_groups(SIZES_MANY, count, *arrays)

    def one_return(p, carry):
        sides = []
        for c in range(2):
            here = slot_place[2 * p + c]
            sides.append(pltpu.roll(grad[here >> 1], ((here & 1) ^ c) * SUB, axis=1))
        picked = jnp.where(lower, sides[0], sides[1])
        out[p] = jnp.where(shades[p] > 0.0, picked, 0.0).astype(jnp.bfloat16)
        return carry

    lax.fori_loop(0, peers, one_return, 0, unroll=8)


def all_but(size):
    return pltpu.CompilerParams(vmem_limit_bytes=max(VMEM - size - 64 * 1024, VMEM_LIMIT))


def round_up(value, step):
    return -(-value // step) * step


def wave_call(wavelengths, tables, message, lenses, extent):
    peers = message.shape[0]
    pairs = max(round_up(lenses, 2 * sum(SIZES_MANY)) // 2, sum(SIZES[-1]))
    vmem = pl.BlockSpec(memory_space=pltpu.VMEM)
    far = pl.BlockSpec(memory_space=pltpu.HBM)
    return pl.pallas_call(
        functools.partial(wave_kernel, lenses),
        out_shape=jax.ShapeDtypeStruct((peers, SUB, LANES), jnp.bfloat16),
        in_specs=[pl.BlockSpec(memory_space=pl.ANY), vmem, far],
        out_specs=vmem,
        scratch_shapes=[
            pltpu.SMEM(wavelengths.shape, jnp.float32),
            pltpu.VMEM((slab_rows(wavelengths.shape[0], lenses), 2 * LANES), jnp.bfloat16),
            pltpu.VMEM((wavelengths.shape[0], 8, LANES), jnp.float32),
            pltpu.VMEM((peers, LANES), jnp.int32),
            pltpu.SMEM((peers, LANES), jnp.int32),
            pltpu.SMEM((lenses,), jnp.int32),
            pltpu.SMEM((2 * peers,), jnp.int32),
            pltpu.SMEM((2 * pairs + 1,), jnp.int32),
            pltpu.VMEM((pairs + 1, SUB, LANES), jnp.float32),
            pltpu.VMEM((pairs + 1, SUB, LANES), jnp.float32),
            pltpu.VMEM((pairs + 1, SUB, LANES), jnp.float32),
            pltpu.VMEM((peers, SUB, LANES), jnp.float32),
            pltpu.VMEM((extent, extent), jnp.float32),
            pltpu.SemaphoreType.DMA,
            pltpu.SemaphoreType.DMA,
            pltpu.SemaphoreType.DMA,
        ],
        compiler_params=pltpu.CompilerParams(vmem_limit_bytes=VMEM_LIMIT),
        name="wave_gradients",
    )(wavelengths, message, tables)


def place_kernel(entries, patches, out, table, sem):
    peers = patches.shape[0]
    extent = out.shape[1]
    copy = pltpu.make_async_copy(entries, table, sem)
    copy.start()
    lane = lax.broadcasted_iota(jnp.int32, (1, LANES), 1)
    spare = jnp.zeros((WINDOW - SUB, LANES), jnp.float32)
    out[...] = jnp.zeros_like(out)
    copy.wait()

    def one_peer(p, carry):
        both = jnp.concatenate([patches[p].astype(jnp.float32), spare], axis=0)
        for c in range(2):
            seg, row, col = (table[k, c, p] for k in (1, 3, 4))
            base, down = aligned(row, extent)
            moved = pltpu.roll(both, (col + LANES - SUB * c) & (LANES - 1), axis=1)
            moved = pltpu.roll(moved, down, axis=0)
            sides = []
            for half in range(2):
                j = lane + (half * LANES - col)
                sides.append(moved * ((j >= 0) & (j < SUB)).astype(jnp.float32))
            out[seg, pl.ds(base, WINDOW), :] += jnp.concatenate(sides, axis=1)
        return carry

    lax.fori_loop(0, peers, one_peer, 0, unroll=4)


def on_device(segment_maps, cotangent, wavelengths, intersections):
    peers = intersections.shape[0]
    segs, extent, _ = segment_maps.shape
    vmem = pl.BlockSpec(memory_space=pltpu.VMEM)
    entries = jnp.transpose(intersections, (2, 1, 0))
    table_shape = (HEAD_ROWS, round_up(peers, LANES))
    table_space = [pltpu.VMEM(table_shape, jnp.int32), pltpu.SMEM(table_shape, jnp.int32)]
    params = pltpu.CompilerParams(vmem_limit_bytes=VMEM_LIMIT)

    message = pl.pallas_call(
        cut_kernel,
        out_shape=jax.ShapeDtypeStruct((peers, SUB + HEAD, LANES), jnp.bfloat16),
        in_specs=[pl.BlockSpec(memory_space=pl.ANY)] * 2,
        out_specs=pl.BlockSpec(memory_space=pltpu.HBM),
        scratch_shapes=[
            pltpu.VMEM(entries.shape, jnp.int32),
            *table_space,
            pltpu.VMEM((segs, extent, extent), jnp.bfloat16),
            pltpu.VMEM((segs, extent, extent), jnp.float32),
            pltpu.VMEM((peers, SUB + HEAD, LANES), jnp.bfloat16),
            pltpu.SemaphoreType.DMA,
            pltpu.SemaphoreType.DMA((segs,)),
            pltpu.SemaphoreType.DMA((peers // math.gcd(peers, BATCH),)),
        ],
        compiler_params=all_but(peers * (SUB + HEAD) * LANES * 2),
        name="cut_patches",
    )(entries, segment_maps)
    tables = table_call(wavelengths, cotangent)
    arriving = lax.all_to_all(message, "tile", split_axis=0, concat_axis=0, tiled=True)
    grads = wave_call(wavelengths, tables, arriving, cotangent.shape[0], extent)
    returned = lax.all_to_all(grads, "tile", split_axis=0, concat_axis=0, tiled=True)
    return pl.pallas_call(
        place_kernel,
        out_shape=jax.ShapeDtypeStruct((segs, extent, extent), jnp.float32),
        in_specs=[pl.BlockSpec(memory_space=pl.ANY), vmem],
        out_specs=vmem,
        scratch_shapes=[pltpu.SMEM(entries.shape, jnp.int32), pltpu.SemaphoreType.DMA],
        compiler_params=params,
        name="place_gradients",
    )(entries, returned)


def solution(mesh):
    return jax.shard_map(
        on_device,
        mesh=mesh,
        in_specs=(
            P(("case", "tile"), None, None),
            P(("case", "tile"), None, None),
            P(),
            P(("case", "tile"), None, None),
        ),
        out_specs=P(("case", "tile"), None, None),
        check_vma=False,
    )
```

```python
import functools
import math

import jax
import jax.numpy as jnp
from jax import lax
from jax.experimental import pallas as pl
from jax.experimental.pallas import tpu as pltpu
from jax.sharding import PartitionSpec as P

SUB = 64
LANES = 2 * SUB
HEAD = 8
HEAD_ROWS = 16
WINDOW = SUB + 8
RIGHT1, RIGHT2, LEFT, WAVE_ROWS = 0, 2 * LANES, 4 * LANES, 5 * LANES
FIELDS = 5
SAMPLING = 0.5
SIZES = ((5,), (4, 3), (5, 4), (5, 5))
SIZES_MANY = (4,)
BATCH = 8
VMEM = 64 * 1024 * 1024
VMEM_LIMIT = 48 * 1024 * 1024
FAR_ROWS = 40960

LEAD = -0.7843722149521581
SINE = tuple(a / LEAD for a in (4.442867901299065, -7.307443351304121, 3.594787401596918))
COSINE = tuple(a / LEAD for a in (1.4142040792740376, -6.9776419299271595, 5.715236658714806, -1.7283430271755356))


FINE_SINE = (4.442882834139933, -7.308241153900929, 3.6062889473067714, -0.8457635292158341, 0.10920561913977103)
FINE_COSINE = (1.4142134965588182, -6.978850987079529, 5.739461141869117, -1.8835627683436942, 0.3106976855933321)


def horner(coefficients, z):
    total = coefficients[-1]
    for coefficient in coefficients[-2::-1]:
        total = total * z + coefficient
    return total


def half_turn(turns):
    r = turns - jnp.round(turns)
    z = r * r
    sine = (((z + SINE[2]) * z + SINE[1]) * z + SINE[0]) * r
    cosine = ((COSINE[3] * z + COSINE[2]) * z + COSINE[1]) * z + COSINE[0]
    return sine, cosine


def row_limit(rows, first, extent):
    i = lax.broadcasted_iota(jnp.int32, (rows, LANES), 0) + first
    down = jnp.abs(2 * i - (extent - 1))
    return jnp.where(8 * down <= 7 * (extent - 1), 7 * (extent - 1) - 4 * down, -1)


def aligned(row, extent):
    base = pl.multiple_of(jnp.minimum(row // 8 * 8, extent - WINDOW), 8)
    return base, row - base


def sideways(first, extent):
    j = lax.broadcasted_iota(jnp.int32, (1, LANES), 1) + first
    return 7 * jnp.abs(2 * j - (extent - 1))


def window(image, row, col, extent, side):
    base, down = aligned(row, extent)
    left = image[pl.ds(base, WINDOW), pl.ds(0, LANES)]
    right = image[pl.ds(base, WINDOW), pl.ds(LANES, LANES)]
    lane = lax.broadcasted_iota(jnp.int32, (WINDOW, LANES), 1)
    both = jnp.where(lane >= col, left, right)
    both = pltpu.roll(both, jnp.where(down == 0, 0, WINDOW - down), axis=0)[:SUB]
    return pltpu.roll(both, (2 * LANES + SUB * side - col) & (LANES - 1), axis=1)


def fill_mask(mask):
    extent = mask.shape[0]
    chunk = 32
    for row in range(0, extent, chunk):
        limit = row_limit(chunk, row, extent)
        for half in range(extent // LANES):
            inside = sideways(half * LANES, extent) <= limit
            mask[pl.ds(row, chunk), pl.ds(half * LANES, LANES)] = jnp.where(inside, 1.0, 0.0)


def read_table(entries, heads, table, sem):
    for k in range(FIELDS):
        heads[pl.ds(2 * k, 2), pl.ds(0, entries.shape[2])] = entries[k]
    copy = pltpu.make_async_copy(heads, table, sem)
    copy.start()
    return copy


def cut_kernel(entries_far, maps, out_far, entries, heads, table, raw, masked, out, sem, map_sems, out_sems):
    peers = out.shape[0]
    segs, extent, _ = maps.shape
    first = pltpu.make_async_copy(entries_far, entries, sem)
    first.start()
    loads = [pltpu.make_async_copy(maps.at[s], raw.at[s], map_sems.at[s]) for s in range(segs)]
    for load in loads:
        load.start()
    lower = lax.broadcasted_iota(jnp.int32, (SUB, LANES), 1) < SUB
    first.wait()
    copy = read_table(entries, heads, table, sem)
    rows = jnp.transpose(heads[...].astype(jnp.float32)).astype(jnp.bfloat16)
    for p in range(peers):
        out[p, pl.ds(SUB, 1), pl.ds(0, HEAD_ROWS)] = rows[p : p + 1]
    for load in loads:
        load.wait()
    chunk = 32
    for row in range(0, extent, chunk):
        limit = row_limit(chunk, row, extent)
        for half in range(extent // LANES):
            inside = sideways(half * LANES, extent) <= limit
            for s in range(segs):
                spot = (s, pl.ds(row, chunk), pl.ds(half * LANES, LANES))
                masked[spot] = jnp.where(inside, raw[spot].astype(jnp.float32), 0.0)
    copy.wait()

    def one_peer(p, carry):
        sides = []
        for c in range(2):
            live, seg, row, col = (table[2 * k + c, p] for k in (0, 1, 3, 4))
            piece = window(masked.at[seg], row, col, extent, c)
            sides.append(piece * live.astype(jnp.float32))
        out[p, pl.ds(0, SUB), :] = jnp.where(lower, sides[0], sides[1]).astype(jnp.bfloat16)
        return carry

    batches = out_sems.shape[0]
    batch = peers // batches

    def send(b):
        part = pl.ds(b * batch, batch)
        return pltpu.make_async_copy(out.at[part], out_far.at[part], out_sems.at[b])

    for b in range(batches):
        lax.fori_loop(b * batch, (b + 1) * batch, one_peer, 0, unroll=True)
        send(b).start()
    for b in range(batches):
        send(b).wait()


def slab_rows(waves, lenses):
    return waves * WAVE_ROWS + round_up(lenses, 2) // 2 * SUB


def weight_spot(lens, waves):
    return pl.ds(waves * WAVE_ROWS + (lens >> 1) * SUB, SUB), pl.ds(pl.multiple_of((lens & 1) * LANES, LANES), LANES)


def table_kernel(waves_ref, cotangent, slab_far, slab, sem):
    waves = waves_ref.shape[0]
    position = lax.broadcasted_iota(jnp.int32, (SUB, LANES), 0) - SUB // 2
    lane = lax.broadcasted_iota(jnp.int32, (SUB, LANES), 1)
    across = (lane & (SUB - 1)) - SUB // 2
    product = (position * across).astype(jnp.float32) * (-SAMPLING / SUB)
    lower = lane < SUB

    def one_table(w, carry):
        turns = product * (1.0 / jnp.full((1, LANES), waves_ref[w], jnp.float32))
        r = turns - jnp.round(turns)
        z = r * r
        sine = horner(FINE_SINE, z) * r
        real = 1.0 - sine * sine
        imag = sine * horner(FINE_COSINE, z)

        def put(row, side, value):
            slab[pl.ds(w * WAVE_ROWS + row, SUB), pl.ds(side * LANES, LANES)] = value.astype(jnp.bfloat16)

        put(LEFT, 0, jnp.where(lower, real, -imag))
        put(LEFT + SUB, 0, jnp.where(lower, imag, real))
        put(LEFT, 1, jnp.where(lower, real, imag))
        put(LEFT + SUB, 1, jnp.where(lower, -imag, real))
        for h in range(2):
            own = lower if h == 0 else ~lower
            re = jnp.where(own, real, 0.0)
            im = jnp.where(own, imag, 0.0)
            first, second = h * SUB, LANES + h * SUB
            put(RIGHT1 + first, 0, re)
            put(RIGHT1 + first, 1, im)
            put(RIGHT1 + second, 0, -im)
            put(RIGHT1 + second, 1, re)
            put(RIGHT2 + first, 0, re)
            put(RIGHT2 + first, 1, -im)
            put(RIGHT2 + second, 0, im)
            put(RIGHT2 + second, 1, re)
        return carry

    lax.fori_loop(0, waves, one_table, 0)
    for l in range(cotangent.shape[0]):
        own = cotangent[l].astype(jnp.float32) * (2.0 / (waves * SUB))
        slab[weight_spot(l, waves)] = jnp.concatenate([own, own], axis=1).astype(jnp.bfloat16)
    copy = pltpu.make_async_copy(slab, slab_far.at[pl.ds(0, slab.shape[0]), :], sem)
    copy.start()
    copy.wait()


def table_call(wavelengths, cotangent):
    vmem = pl.BlockSpec(memory_space=pltpu.VMEM)
    rows = slab_rows(wavelengths.shape[0], cotangent.shape[0])
    return pl.pallas_call(
        table_kernel,
        out_shape=jax.ShapeDtypeStruct((max(rows, FAR_ROWS), 2 * LANES), jnp.bfloat16),
        in_specs=[pl.BlockSpec(memory_space=pltpu.SMEM), vmem],
        out_specs=pl.BlockSpec(memory_space=pltpu.HBM),
        scratch_shapes=[pltpu.VMEM((rows, 2 * LANES), jnp.bfloat16), pltpu.SemaphoreType.DMA],
        compiler_params=pltpu.CompilerParams(vmem_limit_bytes=VMEM_LIMIT),
        cost_estimate=pl.CostEstimate(flops=10_000_000, bytes_accessed=6_000_000, transcendentals=0),
        name="lens_tables",
    )(wavelengths, cotangent)


def wave_groups(sizes, count, owner_of, opd, amplitude, grad, turns_per, slab):
    waves = turns_per.shape[0]
    lower = lax.broadcasted_iota(jnp.int32, (SUB, LANES), 1) < SUB

    def stack(res, ims):
        top = jnp.concatenate([x.astype(jnp.bfloat16) for x in res], axis=1)
        low = jnp.concatenate([x.astype(jnp.bfloat16) for x in ims], axis=1)
        return jnp.concatenate([top, low], axis=0)

    def line(x):
        x = x.astype(jnp.bfloat16)
        rows = []
        for i in range(x.shape[1] // LANES):
            at = slice(LANES * i, LANES * (i + 1))
            rows.append(jnp.concatenate([x[:SUB, at], x[SUB:, at]], axis=1))
        return jnp.concatenate(rows, axis=0)

    def begin(start, size):
        weights, scaled = [], []
        for i in range(size):
            k = (start + i) * 2
            scaled.append(amplitude[start + i] * LEAD**2)
            pieces = [slab[weight_spot(owner_of[k + h], waves)].astype(jnp.float32) for h in range(2)]
            weights.append(jnp.where(lower, *pieces))
        return start, weights, scaled, [None] * size

    def field(w, own, state):
        start, _, scaled, _ = own
        scale = turns_per[w][0:1]
        reals, imags = [], []
        for i in range(len(scaled)):
            sine, cosine = half_turn(opd[start + i] * scale)
            part = scaled[i] * sine
            reals.append(amplitude[start + i] - part * sine)
            imags.append(part * cosine)
        return reals, imags, stack(reals, imags)

    def pupil_rows(w, own, state):
        reals, imags, e = state
        table = slab[pl.ds(w * WAVE_ROWS + LEFT, LANES), pl.ds(0, LANES)]
        return reals, imags, line(jnp.dot(table, e, preferred_element_type=jnp.float32))

    def pupil_columns(w, own, state):
        reals, imags, p = state
        weights = own[1]
        table = slab[pl.ds(w * WAVE_ROWS + RIGHT1, 2 * LANES), :]
        f = jnp.dot(p, table, preferred_element_type=jnp.float32)
        held = [[], []]
        for i in range(len(weights)):
            for h in range(2):
                held[h].append(f[SUB * i : SUB * (i + 1), LANES * h : LANES * (h + 1)] * weights[i])
        return reals, imags, stack(*held)

    def focal_rows(w, own, state):
        reals, imags, held = state
        table = slab[pl.ds(w * WAVE_ROWS + LEFT, LANES), pl.ds(LANES, LANES)]
        return reals, imags, line(jnp.dot(table, held, preferred_element_type=jnp.float32))

    def focal_columns(w, own, state):
        reals, imags, q = state
        start, _, _, totals = own
        table = slab[pl.ds(w * WAVE_ROWS + RIGHT2, 2 * LANES), :]
        b = jnp.dot(q, table, preferred_element_type=jnp.float32)
        factor = turns_per[w][0:1] * (2.0 * math.pi / SUB)
        for i in range(len(totals)):
            back = b[SUB * i : SUB * (i + 1)]
            term = factor * (reals[i] * back[:, LANES:] - imags[i] * back[:, :LANES])
            totals[i] = term if totals[i] is None else totals[i] + term
            if w == waves - 1:
                grad[start + i] = totals[i]

    stages = (field, pupil_rows, pupil_columns, focal_rows, focal_columns)

    def some_groups(turn, carry):
        owns, states = {}, {}
        items = len(sizes) * waves
        for t in range(items + len(stages) - 1):
            for k, stage in enumerate(stages):
                n = t - k
                if 0 <= n < items:
                    g, w = divmod(n, waves)
                    if g not in owns:
                        owns[g] = begin(turn * sum(sizes) + sum(sizes[:g]), sizes[g])
                    states[n] = stage(w, owns[g], states.pop(n, None))
        return carry

    step = 2 * sum(sizes)
    lax.fori_loop(0, (count + step - 1) // step, some_groups, 0)


def wave_kernel(
    lenses, waves_far, message, slab_far, out,
    waves_ref, slab, turns_per, heads, table, place, slot_place, owner_of, opd, amplitude, grad, shades, mask, sem, slab_sem, waves_sem,
):
    peers = message.shape[0]
    pairs = opd.shape[0] - 1
    extent = mask.shape[0]
    dead_place = 2 * pairs

    load = pltpu.make_async_copy(slab_far.at[pl.ds(0, slab.shape[0]), :], slab, slab_sem)
    load.start()
    waves_load = pltpu.make_async_copy(waves_far, waves_ref, waves_sem)
    waves_load.start()
    for p in range(peers):
        head = message[p, pl.ds(SUB, HEAD), :].astype(jnp.float32)[0:1]
        heads[pl.ds(p, 1), :] = head.astype(jnp.int32)
    copy = pltpu.make_async_copy(heads, table, sem)
    copy.start()
    fill_mask(mask)
    opd[...] = jnp.zeros_like(opd)
    amplitude[...] = jnp.zeros_like(amplitude)
    lane = lax.broadcasted_iota(jnp.int32, (SUB, LANES), 1)
    lower = lane < SUB
    row_lane = lax.broadcasted_iota(jnp.int32, (1, LANES), 1) >> 6
    for l in range(lenses):
        place[l] = -1
    for k in range(dead_place + 1):
        owner_of[k] = 0
    copy.wait()

    def one_slot(p, count):
        patch = message[p, pl.ds(0, SUB), :].astype(jnp.float32)
        sides, heres = [], []
        for c in range(2):
            live, lens, row, col = (table[p, 2 * k + c] for k in (0, 2, 3, 4))
            sides.append(window(mask, row, col, extent, c) * live.astype(jnp.float32))
            before = place[lens]
            fresh = (live == 1) & (before < 0)
            here = jnp.where(fresh, count, before)
            place[lens] = here
            owner_of[count] = jnp.where(fresh, lens, 0)
            count = count + fresh.astype(jnp.int32)
            heres.append(jnp.where(live == 1, here, dead_place))
            slot_place[2 * p + c] = heres[c]
        shade = jnp.where(lower, sides[0], sides[1])
        shades[p] = shade
        for c in range(2):
            pair = heres[c] >> 1
            half = heres[c] & 1
            turn = (half ^ c) * SUB
            own = (row_lane == half).astype(jnp.float32)
            opd[pair] += pltpu.roll(patch, turn, axis=1) * own
            amplitude[pair] += pltpu.roll(shade, turn, axis=1) * own
        return count

    count = lax.fori_loop(0, peers, one_slot, 0, unroll=16)
    waves_load.wait()
    for w in range(waves_ref.shape[0]):
        turns_per[w] = 1.0 / jnp.full((8, LANES), waves_ref[w], jnp.float32)
    load.wait()

    arrays = (owner_of, opd, amplitude, grad, turns_per, slab)
    floor = 0
    for sizes in SIZES:
        ceiling = 2 * sum(sizes)

        @pl.when((count > floor) & (count <= ceiling))
        def _(sizes=sizes):
            wave_groups(sizes, count, *arrays)

        floor = ceiling

    @pl.when(count > floor)
    def _():
        wave_groups(SIZES_MANY, count, *arrays)

    def one_return(p, carry):
        sides = []
        for c in range(2):
            here = slot_place[2 * p + c]
            sides.append(pltpu.roll(grad[here >> 1], ((here & 1) ^ c) * SUB, axis=1))
        picked = jnp.where(lower, sides[0], sides[1])
        out[p] = jnp.where(shades[p] > 0.0, picked, 0.0).astype(jnp.bfloat16)
        return carry

    lax.fori_loop(0, peers, one_return, 0, unroll=8)


def all_but(size):
    return pltpu.CompilerParams(vmem_limit_bytes=max(VMEM - size - 64 * 1024, VMEM_LIMIT))


def round_up(value, step):
    return -(-value // step) * step


def wave_call(wavelengths, tables, message, lenses, extent):
    peers = message.shape[0]
    pairs = max(round_up(lenses, 2 * sum(SIZES_MANY)) // 2, sum(SIZES[-1]))
    vmem = pl.BlockSpec(memory_space=pltpu.VMEM)
    far = pl.BlockSpec(memory_space=pltpu.HBM)
    return pl.pallas_call(
        functools.partial(wave_kernel, lenses),
        out_shape=jax.ShapeDtypeStruct((peers, SUB, LANES), jnp.bfloat16),
        in_specs=[pl.BlockSpec(memory_space=pl.ANY), vmem, far],
        out_specs=vmem,
        scratch_shapes=[
            pltpu.SMEM(wavelengths.shape, jnp.float32),
            pltpu.VMEM((slab_rows(wavelengths.shape[0], lenses), 2 * LANES), jnp.bfloat16),
            pltpu.VMEM((wavelengths.shape[0], 8, LANES), jnp.float32),
            pltpu.VMEM((peers, LANES), jnp.int32),
            pltpu.SMEM((peers, LANES), jnp.int32),
            pltpu.SMEM((lenses,), jnp.int32),
            pltpu.SMEM((2 * peers,), jnp.int32),
            pltpu.SMEM((2 * pairs + 1,), jnp.int32),
            pltpu.VMEM((pairs + 1, SUB, LANES), jnp.float32),
            pltpu.VMEM((pairs + 1, SUB, LANES), jnp.float32),
            pltpu.VMEM((pairs + 1, SUB, LANES), jnp.float32),
            pltpu.VMEM((peers, SUB, LANES), jnp.float32),
            pltpu.VMEM((extent, extent), jnp.float32),
            pltpu.SemaphoreType.DMA,
            pltpu.SemaphoreType.DMA,
            pltpu.SemaphoreType.DMA,
        ],
        compiler_params=pltpu.CompilerParams(vmem_limit_bytes=VMEM_LIMIT),
        name="wave_gradients",
    )(wavelengths, message, tables)


def place_kernel(entries, patches, out, table, sem):
    peers = patches.shape[0]
    extent = out.shape[1]
    copy = pltpu.make_async_copy(entries, table, sem)
    copy.start()
    lane = lax.broadcasted_iota(jnp.int32, (1, LANES), 1)
    spare = jnp.zeros((WINDOW - SUB, LANES), jnp.float32)
    out[...] = jnp.zeros_like(out)
    copy.wait()

    def one_peer(p, carry):
        both = jnp.concatenate([patches[p].astype(jnp.float32), spare], axis=0)
        for c in range(2):
            seg, row, col = (table[k, c, p] for k in (1, 3, 4))
            base, down = aligned(row, extent)
            moved = pltpu.roll(both, (col + LANES - SUB * c) & (LANES - 1), axis=1)
            moved = pltpu.roll(moved, down, axis=0)
            sides = []
            for half in range(2):
                j = lane + (half * LANES - col)
                sides.append(moved * ((j >= 0) & (j < SUB)).astype(jnp.float32))
            out[seg, pl.ds(base, WINDOW), :] += jnp.concatenate(sides, axis=1)
        return carry

    lax.fori_loop(0, peers, one_peer, 0, unroll=16)


def on_device(segment_maps, cotangent, wavelengths, intersections):
    peers = intersections.shape[0]
    segs, extent, _ = segment_maps.shape
    vmem = pl.BlockSpec(memory_space=pltpu.VMEM)
    entries = jnp.transpose(intersections, (2, 1, 0))
    table_shape = (HEAD_ROWS, round_up(peers, LANES))
    table_space = [pltpu.VMEM(table_shape, jnp.int32), pltpu.SMEM(table_shape, jnp.int32)]
    params = pltpu.CompilerParams(vmem_limit_bytes=VMEM_LIMIT)

    message = pl.pallas_call(
        cut_kernel,
        out_shape=jax.ShapeDtypeStruct((peers, SUB + HEAD, LANES), jnp.bfloat16),
        in_specs=[pl.BlockSpec(memory_space=pl.ANY)] * 2,
        out_specs=pl.BlockSpec(memory_space=pltpu.HBM),
        scratch_shapes=[
            pltpu.VMEM(entries.shape, jnp.int32),
            *table_space,
            pltpu.VMEM((segs, extent, extent), jnp.bfloat16),
            pltpu.VMEM((segs, extent, extent), jnp.float32),
            pltpu.VMEM((peers, SUB + HEAD, LANES), jnp.bfloat16),
            pltpu.SemaphoreType.DMA,
            pltpu.SemaphoreType.DMA((segs,)),
            pltpu.SemaphoreType.DMA((peers // math.gcd(peers, BATCH),)),
        ],
        compiler_params=all_but(peers * (SUB + HEAD) * LANES * 2),
        name="cut_patches",
    )(entries, segment_maps)
    tables = table_call(wavelengths, cotangent)
    arriving = lax.all_to_all(message, "tile", split_axis=0, concat_axis=0, tiled=True)
    grads = wave_call(wavelengths, tables, arriving, cotangent.shape[0], extent)
    returned = lax.all_to_all(grads, "tile", split_axis=0, concat_axis=0, tiled=True)
    return pl.pallas_call(
        place_kernel,
        out_shape=jax.ShapeDtypeStruct((segs, extent, extent), jnp.float32),
        in_specs=[pl.BlockSpec(memory_space=pl.ANY), vmem],
        out_specs=vmem,
        scratch_shapes=[pltpu.SMEM(entries.shape, jnp.int32), pltpu.SemaphoreType.DMA],
        compiler_params=params,
        name="place_gradients",
    )(entries, returned)


def solution(mesh):
    return jax.shard_map(
        on_device,
        mesh=mesh,
        in_specs=(
            P(("case", "tile"), None, None),
            P(("case", "tile"), None, None),
            P(),
            P(("case", "tile"), None, None),
        ),
        out_specs=P(("case", "tile"), None, None),
        check_vma=False,
    )
```

```python
import functools
import math

import jax
import jax.numpy as jnp
from jax import lax
from jax.experimental import pallas as pl
from jax.experimental.pallas import tpu as pltpu
from jax.sharding import PartitionSpec as P

SUB = 64
LANES = 2 * SUB
HEAD = 8
HEAD_ROWS = 16
WINDOW = SUB + 8
RIGHT1, RIGHT2, LEFT, WAVE_ROWS = 0, 2 * LANES, 4 * LANES, 5 * LANES
FIELDS = 5
SAMPLING = 0.5
SIZES = ((5,), (4, 3), (5, 4), (5, 5))
SIZES_MANY = (4,)
BATCH = 4
VMEM = 64 * 1024 * 1024
VMEM_LIMIT = 48 * 1024 * 1024
FAR_ROWS = 40960

LEAD = -0.7843722149521581
SINE = tuple(a / LEAD for a in (4.442867901299065, -7.307443351304121, 3.594787401596918))
COSINE = tuple(a / LEAD for a in (1.4142040792740376, -6.9776419299271595, 5.715236658714806, -1.7283430271755356))


FINE_SINE = (4.442882834139933, -7.308241153900929, 3.6062889473067714, -0.8457635292158341, 0.10920561913977103)
FINE_COSINE = (1.4142134965588182, -6.978850987079529, 5.739461141869117, -1.8835627683436942, 0.3106976855933321)


def horner(coefficients, z):
    total = coefficients[-1]
    for coefficient in coefficients[-2::-1]:
        total = total * z + coefficient
    return total


def half_turn(turns):
    r = turns - jnp.round(turns)
    z = r * r
    sine = (((z + SINE[2]) * z + SINE[1]) * z + SINE[0]) * r
    cosine = ((COSINE[3] * z + COSINE[2]) * z + COSINE[1]) * z + COSINE[0]
    return sine, cosine


def row_limit(rows, first, extent):
    i = lax.broadcasted_iota(jnp.int32, (rows, LANES), 0) + first
    down = jnp.abs(2 * i - (extent - 1))
    return jnp.where(8 * down <= 7 * (extent - 1), 7 * (extent - 1) - 4 * down, -1)


def aligned(row, extent):
    base = pl.multiple_of(jnp.minimum(row // 8 * 8, extent - WINDOW), 8)
    return base, row - base


def sideways(first, extent):
    j = lax.broadcasted_iota(jnp.int32, (1, LANES), 1) + first
    return 7 * jnp.abs(2 * j - (extent - 1))


def window(image, row, col, extent, side):
    base, down = aligned(row, extent)
    left = image[pl.ds(base, WINDOW), pl.ds(0, LANES)]
    right = image[pl.ds(base, WINDOW), pl.ds(LANES, LANES)]
    lane = lax.broadcasted_iota(jnp.int32, (WINDOW, LANES), 1)
    both = jnp.where(lane >= col, left, right)
    both = pltpu.roll(both, jnp.where(down == 0, 0, WINDOW - down), axis=0)[:SUB]
    return pltpu.roll(both, (2 * LANES + SUB * side - col) & (LANES - 1), axis=1)


def fill_mask(mask):
    extent = mask.shape[0]
    chunk = 32
    for row in range(0, extent, chunk):
        limit = row_limit(chunk, row, extent)
        for half in range(extent // LANES):
            inside = sideways(half * LANES, extent) <= limit
            mask[pl.ds(row, chunk), pl.ds(half * LANES, LANES)] = jnp.where(inside, 1.0, 0.0)


def read_table(entries, heads, table, sem):
    for k in range(FIELDS):
        heads[pl.ds(2 * k, 2), pl.ds(0, entries.shape[2])] = entries[k]
    copy = pltpu.make_async_copy(heads, table, sem)
    copy.start()
    return copy


def cut_kernel(entries_far, maps, out_far, entries, heads, table, raw, masked, out, sem, map_sems, out_sems):
    peers = out.shape[0]
    segs, extent, _ = maps.shape
    first = pltpu.make_async_copy(entries_far, entries, sem)
    first.start()
    loads = [pltpu.make_async_copy(maps.at[s], raw.at[s], map_sems.at[s]) for s in range(segs)]
    for load in loads:
        load.start()
    lower = lax.broadcasted_iota(jnp.int32, (SUB, LANES), 1) < SUB
    first.wait()
    copy = read_table(entries, heads, table, sem)
    rows = jnp.transpose(heads[...].astype(jnp.float32)).astype(jnp.bfloat16)
    for p in range(peers):
        out[p, pl.ds(SUB, 1), pl.ds(0, HEAD_ROWS)] = rows[p : p + 1]
    for load in loads:
        load.wait()
    chunk = 32
    for row in range(0, extent, chunk):
        limit = row_limit(chunk, row, extent)
        for half in range(extent // LANES):
            inside = sideways(half * LANES, extent) <= limit
            for s in range(segs):
                spot = (s, pl.ds(row, chunk), pl.ds(half * LANES, LANES))
                masked[spot] = jnp.where(inside, raw[spot].astype(jnp.float32), 0.0)
    copy.wait()

    def one_peer(p, carry):
        sides = []
        for c in range(2):
            live, seg, row, col = (table[2 * k + c, p] for k in (0, 1, 3, 4))
            piece = window(masked.at[seg], row, col, extent, c)
            sides.append(piece * live.astype(jnp.float32))
        out[p, pl.ds(0, SUB), :] = jnp.where(lower, sides[0], sides[1]).astype(jnp.bfloat16)
        return carry

    batches = out_sems.shape[0]
    batch = peers // batches

    def send(b):
        part = pl.ds(b * batch, batch)
        return pltpu.make_async_copy(out.at[part], out_far.at[part], out_sems.at[b])

    for b in range(batches):
        lax.fori_loop(b * batch, (b + 1) * batch, one_peer, 0, unroll=True)
        send(b).start()
    for b in range(batches):
        send(b).wait()


def slab_rows(waves, lenses):
    return waves * WAVE_ROWS + round_up(lenses, 2) // 2 * SUB


def weight_spot(lens, waves):
    return pl.ds(waves * WAVE_ROWS + (lens >> 1) * SUB, SUB), pl.ds(pl.multiple_of((lens & 1) * LANES, LANES), LANES)


def table_kernel(waves_ref, cotangent, slab_far, slab, sem):
    waves = waves_ref.shape[0]
    position = lax.broadcasted_iota(jnp.int32, (SUB, LANES), 0) - SUB // 2
    lane = lax.broadcasted_iota(jnp.int32, (SUB, LANES), 1)
    across = (lane & (SUB - 1)) - SUB // 2
    product = (position * across).astype(jnp.float32) * (-SAMPLING / SUB)
    lower = lane < SUB

    def one_table(w, carry):
        turns = product * (1.0 / jnp.full((1, LANES), waves_ref[w], jnp.float32))
        r = turns - jnp.round(turns)
        z = r * r
        sine = horner(FINE_SINE, z) * r
        real = 1.0 - sine * sine
        imag = sine * horner(FINE_COSINE, z)

        def put(row, side, value):
            slab[pl.ds(w * WAVE_ROWS + row, SUB), pl.ds(side * LANES, LANES)] = value.astype(jnp.bfloat16)

        put(LEFT, 0, jnp.where(lower, real, -imag))
        put(LEFT + SUB, 0, jnp.where(lower, imag, real))
        put(LEFT, 1, jnp.where(lower, real, imag))
        put(LEFT + SUB, 1, jnp.where(lower, -imag, real))
        for h in range(2):
            own = lower if h == 0 else ~lower
            re = jnp.where(own, real, 0.0)
            im = jnp.where(own, imag, 0.0)
            first, second = h * SUB, LANES + h * SUB
            put(RIGHT1 + first, 0, re)
            put(RIGHT1 + first, 1, im)
            put(RIGHT1 + second, 0, -im)
            put(RIGHT1 + second, 1, re)
            put(RIGHT2 + first, 0, re)
            put(RIGHT2 + first, 1, -im)
            put(RIGHT2 + second, 0, im)
            put(RIGHT2 + second, 1, re)
        return carry

    lax.fori_loop(0, waves, one_table, 0)
    for l in range(cotangent.shape[0]):
        own = cotangent[l].astype(jnp.float32) * (2.0 / (waves * SUB))
        slab[weight_spot(l, waves)] = jnp.concatenate([own, own], axis=1).astype(jnp.bfloat16)
    copy = pltpu.make_async_copy(slab, slab_far.at[pl.ds(0, slab.shape[0]), :], sem)
    copy.start()
    copy.wait()


def table_call(wavelengths, cotangent):
    vmem = pl.BlockSpec(memory_space=pltpu.VMEM)
    rows = slab_rows(wavelengths.shape[0], cotangent.shape[0])
    return pl.pallas_call(
        table_kernel,
        out_shape=jax.ShapeDtypeStruct((max(rows, FAR_ROWS), 2 * LANES), jnp.bfloat16),
        in_specs=[pl.BlockSpec(memory_space=pltpu.SMEM), vmem],
        out_specs=pl.BlockSpec(memory_space=pltpu.HBM),
        scratch_shapes=[pltpu.VMEM((rows, 2 * LANES), jnp.bfloat16), pltpu.SemaphoreType.DMA],
        compiler_params=pltpu.CompilerParams(vmem_limit_bytes=VMEM_LIMIT),
        cost_estimate=pl.CostEstimate(flops=10_000_000, bytes_accessed=6_000_000, transcendentals=0),
        name="lens_tables",
    )(wavelengths, cotangent)


def wave_groups(sizes, count, owner_of, opd, amplitude, grad, turns_per, slab):
    waves = turns_per.shape[0]
    lower = lax.broadcasted_iota(jnp.int32, (SUB, LANES), 1) < SUB

    def stack(res, ims):
        top = jnp.concatenate([x.astype(jnp.bfloat16) for x in res], axis=1)
        low = jnp.concatenate([x.astype(jnp.bfloat16) for x in ims], axis=1)
        return jnp.concatenate([top, low], axis=0)

    def line(x):
        x = x.astype(jnp.bfloat16)
        rows = []
        for i in range(x.shape[1] // LANES):
            at = slice(LANES * i, LANES * (i + 1))
            rows.append(jnp.concatenate([x[:SUB, at], x[SUB:, at]], axis=1))
        return jnp.concatenate(rows, axis=0)

    def begin(start, size):
        weights, scaled = [], []
        for i in range(size):
            k = (start + i) * 2
            scaled.append(amplitude[start + i] * LEAD**2)
            pieces = [slab[weight_spot(owner_of[k + h], waves)].astype(jnp.float32) for h in range(2)]
            weights.append(jnp.where(lower, *pieces))
        return start, weights, scaled, [None] * size

    def field(w, own, state):
        start, _, scaled, _ = own
        scale = turns_per[w][0:1]
        reals, imags = [], []
        for i in range(len(scaled)):
            sine, cosine = half_turn(opd[start + i] * scale)
            part = scaled[i] * sine
            reals.append(amplitude[start + i] - part * sine)
            imags.append(part * cosine)
        return reals, imags, stack(reals, imags)

    def pupil_rows(w, own, state):
        reals, imags, e = state
        table = slab[pl.ds(w * WAVE_ROWS + LEFT, LANES), pl.ds(0, LANES)]
        return reals, imags, line(jnp.dot(table, e, preferred_element_type=jnp.float32))

    def pupil_columns(w, own, state):
        reals, imags, p = state
        weights = own[1]
        table = slab[pl.ds(w * WAVE_ROWS + RIGHT1, 2 * LANES), :]
        f = jnp.dot(p, table, preferred_element_type=jnp.float32)
        held = [[], []]
        for i in range(len(weights)):
            for h in range(2):
                held[h].append(f[SUB * i : SUB * (i + 1), LANES * h : LANES * (h + 1)] * weights[i])
        return reals, imags, stack(*held)

    def focal_rows(w, own, state):
        reals, imags, held = state
        table = slab[pl.ds(w * WAVE_ROWS + LEFT, LANES), pl.ds(LANES, LANES)]
        return reals, imags, line(jnp.dot(table, held, preferred_element_type=jnp.float32))

    def focal_columns(w, own, state):
        reals, imags, q = state
        start, _, _, totals = own
        table = slab[pl.ds(w * WAVE_ROWS + RIGHT2, 2 * LANES), :]
        b = jnp.dot(q, table, preferred_element_type=jnp.float32)
        factor = turns_per[w][0:1] * (2.0 * math.pi / SUB)
        for i in range(len(totals)):
            back = b[SUB * i : SUB * (i + 1)]
            term = factor * (reals[i] * back[:, LANES:] - imags[i] * back[:, :LANES])
            totals[i] = term if totals[i] is None else totals[i] + term
            if w == waves - 1:
                grad[start + i] = totals[i]

    stages = (field, pupil_rows, pupil_columns, focal_rows, focal_columns)

    def some_groups(turn, carry):
        owns, states = {}, {}
        items = len(sizes) * waves
        for t in range(items + len(stages) - 1):
            for k, stage in enumerate(stages):
                n = t - k
                if 0 <= n < items:
                    g, w = divmod(n, waves)
                    if g not in owns:
                        owns[g] = begin(turn * sum(sizes) + sum(sizes[:g]), sizes[g])
                    states[n] = stage(w, owns[g], states.pop(n, None))
        return carry

    step = 2 * sum(sizes)
    lax.fori_loop(0, (count + step - 1) // step, some_groups, 0)


def wave_kernel(
    lenses, waves_far, message, slab_far, out,
    waves_ref, slab, turns_per, heads, table, place, slot_place, owner_of, opd, amplitude, grad, shades, mask, sem, slab_sem, waves_sem,
):
    peers = message.shape[0]
    pairs = opd.shape[0] - 1
    extent = mask.shape[0]
    dead_place = 2 * pairs

    load = pltpu.make_async_copy(slab_far.at[pl.ds(0, slab.shape[0]), :], slab, slab_sem)
    load.start()
    waves_load = pltpu.make_async_copy(waves_far, waves_ref, waves_sem)
    waves_load.start()
    for p in range(peers):
        head = message[p, pl.ds(SUB, HEAD), :].astype(jnp.float32)[0:1]
        heads[pl.ds(p, 1), :] = head.astype(jnp.int32)
    copy = pltpu.make_async_copy(heads, table, sem)
    copy.start()
    fill_mask(mask)
    opd[...] = jnp.zeros_like(opd)
    amplitude[...] = jnp.zeros_like(amplitude)
    lane = lax.broadcasted_iota(jnp.int32, (SUB, LANES), 1)
    lower = lane < SUB
    row_lane = lax.broadcasted_iota(jnp.int32, (1, LANES), 1) >> 6
    for l in range(lenses):
        place[l] = -1
    for k in range(dead_place + 1):
        owner_of[k] = 0
    copy.wait()

    def one_slot(p, count):
        patch = message[p, pl.ds(0, SUB), :].astype(jnp.float32)
        sides, heres = [], []
        for c in range(2):
            live, lens, row, col = (table[p, 2 * k + c] for k in (0, 2, 3, 4))
            sides.append(window(mask, row, col, extent, c) * live.astype(jnp.float32))
            before = place[lens]
            fresh = (live == 1) & (before < 0)
            here = jnp.where(fresh, count, before)
            place[lens] = here
            owner_of[count] = jnp.where(fresh, lens, 0)
            count = count + fresh.astype(jnp.int32)
            heres.append(jnp.where(live == 1, here, dead_place))
            slot_place[2 * p + c] = heres[c]
        shade = jnp.where(lower, sides[0], sides[1])
        shades[p] = shade
        for c in range(2):
            pair = heres[c] >> 1
            half = heres[c] & 1
            turn = (half ^ c) * SUB
            own = (row_lane == half).astype(jnp.float32)
            opd[pair] += pltpu.roll(patch, turn, axis=1) * own
            amplitude[pair] += pltpu.roll(shade, turn, axis=1) * own
        return count

    count = lax.fori_loop(0, peers, one_slot, 0, unroll=16)
    waves_load.wait()
    for w in range(waves_ref.shape[0]):
        turns_per[w] = 1.0 / jnp.full((8, LANES), waves_ref[w], jnp.float32)
    load.wait()

    arrays = (owner_of, opd, amplitude, grad, turns_per, slab)
    floor = 0
    for sizes in SIZES:
        ceiling = 2 * sum(sizes)

        @pl.when((count > floor) & (count <= ceiling))
        def _(sizes=sizes):
            wave_groups(sizes, count, *arrays)

        floor = ceiling

    @pl.when(count > floor)
    def _():
        wave_groups(SIZES_MANY, count, *arrays)

    def one_return(p, carry):
        sides = []
        for c in range(2):
            here = slot_place[2 * p + c]
            sides.append(pltpu.roll(grad[here >> 1], ((here & 1) ^ c) * SUB, axis=1))
        picked = jnp.where(lower, sides[0], sides[1])
        out[p] = jnp.where(shades[p] > 0.0, picked, 0.0).astype(jnp.bfloat16)
        return carry

    lax.fori_loop(0, peers, one_return, 0, unroll=16)


def all_but(size):
    return pltpu.CompilerParams(vmem_limit_bytes=max(VMEM - size - 64 * 1024, VMEM_LIMIT))


def round_up(value, step):
    return -(-value // step) * step


def wave_call(wavelengths, tables, message, lenses, extent):
    peers = message.shape[0]
    pairs = max(round_up(lenses, 2 * sum(SIZES_MANY)) // 2, sum(SIZES[-1]))
    vmem = pl.BlockSpec(memory_space=pltpu.VMEM)
    far = pl.BlockSpec(memory_space=pltpu.HBM)
    return pl.pallas_call(
        functools.partial(wave_kernel, lenses),
        out_shape=jax.ShapeDtypeStruct((peers, SUB, LANES), jnp.bfloat16),
        in_specs=[pl.BlockSpec(memory_space=pl.ANY), vmem, far],
        out_specs=vmem,
        scratch_shapes=[
            pltpu.SMEM(wavelengths.shape, jnp.float32),
            pltpu.VMEM((slab_rows(wavelengths.shape[0], lenses), 2 * LANES), jnp.bfloat16),
            pltpu.VMEM((wavelengths.shape[0], 8, LANES), jnp.float32),
            pltpu.VMEM((peers, LANES), jnp.int32),
            pltpu.SMEM((peers, LANES), jnp.int32),
            pltpu.SMEM((lenses,), jnp.int32),
            pltpu.SMEM((2 * peers,), jnp.int32),
            pltpu.SMEM((2 * pairs + 1,), jnp.int32),
            pltpu.VMEM((pairs + 1, SUB, LANES), jnp.float32),
            pltpu.VMEM((pairs + 1, SUB, LANES), jnp.float32),
            pltpu.VMEM((pairs + 1, SUB, LANES), jnp.float32),
            pltpu.VMEM((peers, SUB, LANES), jnp.float32),
            pltpu.VMEM((extent, extent), jnp.float32),
            pltpu.SemaphoreType.DMA,
            pltpu.SemaphoreType.DMA,
            pltpu.SemaphoreType.DMA,
        ],
        compiler_params=pltpu.CompilerParams(vmem_limit_bytes=VMEM_LIMIT),
        name="wave_gradients",
    )(wavelengths, message, tables)


def place_kernel(entries, patches, out, table, sem):
    peers = patches.shape[0]
    extent = out.shape[1]
    copy = pltpu.make_async_copy(entries, table, sem)
    copy.start()
    lane = lax.broadcasted_iota(jnp.int32, (1, LANES), 1)
    spare = jnp.zeros((WINDOW - SUB, LANES), jnp.float32)
    out[...] = jnp.zeros_like(out)
    copy.wait()

    def one_peer(p, carry):
        both = jnp.concatenate([patches[p].astype(jnp.float32), spare], axis=0)
        for c in range(2):
            seg, row, col = (table[k, c, p] for k in (1, 3, 4))
            base, down = aligned(row, extent)
            moved = pltpu.roll(both, (col + LANES - SUB * c) & (LANES - 1), axis=1)
            moved = pltpu.roll(moved, down, axis=0)
            sides = []
            for half in range(2):
                j = lane + (half * LANES - col)
                sides.append(moved * ((j >= 0) & (j < SUB)).astype(jnp.float32))
            out[seg, pl.ds(base, WINDOW), :] += jnp.concatenate(sides, axis=1)
        return carry

    lax.fori_loop(0, peers, one_peer, 0, unroll=16)


def on_device(segment_maps, cotangent, wavelengths, intersections):
    peers = intersections.shape[0]
    segs, extent, _ = segment_maps.shape
    vmem = pl.BlockSpec(memory_space=pltpu.VMEM)
    entries = jnp.transpose(intersections, (2, 1, 0))
    table_shape = (HEAD_ROWS, round_up(peers, LANES))
    table_space = [pltpu.VMEM(table_shape, jnp.int32), pltpu.SMEM(table_shape, jnp.int32)]
    params = pltpu.CompilerParams(vmem_limit_bytes=VMEM_LIMIT)

    message = pl.pallas_call(
        cut_kernel,
        out_shape=jax.ShapeDtypeStruct((peers, SUB + HEAD, LANES), jnp.bfloat16),
        in_specs=[pl.BlockSpec(memory_space=pl.ANY)] * 2,
        out_specs=pl.BlockSpec(memory_space=pltpu.HBM),
        scratch_shapes=[
            pltpu.VMEM(entries.shape, jnp.int32),
            *table_space,
            pltpu.VMEM((segs, extent, extent), jnp.bfloat16),
            pltpu.VMEM((segs, extent, extent), jnp.float32),
            pltpu.VMEM((peers, SUB + HEAD, LANES), jnp.bfloat16),
            pltpu.SemaphoreType.DMA,
            pltpu.SemaphoreType.DMA((segs,)),
            pltpu.SemaphoreType.DMA((peers // math.gcd(peers, BATCH),)),
        ],
        compiler_params=all_but(peers * (SUB + HEAD) * LANES * 2),
        name="cut_patches",
    )(entries, segment_maps)
    tables = table_call(wavelengths, cotangent)
    arriving = lax.all_to_all(message, "tile", split_axis=0, concat_axis=0, tiled=True)
    grads = wave_call(wavelengths, tables, arriving, cotangent.shape[0], extent)
    returned = lax.all_to_all(grads, "tile", split_axis=0, concat_axis=0, tiled=True)
    return pl.pallas_call(
        place_kernel,
        out_shape=jax.ShapeDtypeStruct((segs, extent, extent), jnp.float32),
        in_specs=[pl.BlockSpec(memory_space=pl.ANY), vmem],
        out_specs=vmem,
        scratch_shapes=[pltpu.SMEM(entries.shape, jnp.int32), pltpu.SemaphoreType.DMA],
        compiler_params=params,
        name="place_gradients",
    )(entries, returned)


def solution(mesh):
    return jax.shard_map(
        on_device,
        mesh=mesh,
        in_specs=(
            P(("case", "tile"), None, None),
            P(("case", "tile"), None, None),
            P(),
            P(("case", "tile"), None, None),
        ),
        out_specs=P(("case", "tile"), None, None),
        check_vma=False,
    )
```
